32 devices in a mesh: sec: 4 (over y, x), dom: 8 (over z, core).
Axes of the slice: x: 2, y: 2, z: 4, core: 2. Of those that a mesh axis runs over, the one named last changes fastest.
Arguments:
- spectrum: bfloat16 [1296, 4096], P(None, ('sec', 'dom')), may hold values from 0.099609375 to 2
- surface_wind: float32 [2, 4096], P(None, ('sec', 'dom')), may hold values from -30 to 30
- wet_mask: float32 [4096], P(('sec', 'dom')), may hold values from 0.5 to 1
- block_order: int32 [32], P(('sec', 'dom')), may hold values from 0 to 7, as said below
Outputs:
- new_spectrum: bfloat16 [1296, 4096], P(None, ('sec', 'dom'))
- wave_stress: float32 [2, 4096], P(None, ('sec', 'dom'))
The draws below stay inside these ranges and needn't reach their ends.
Inputs may be any that keep to these rules, and one draw needn't show every extreme that they name: `block_order`: each aligned block of 8 entries, those of one section, is a permutation of 0 to 7.
All inputs are finite; a program needn't handle non-finite values.
Results may differ from the reference program's by a relative error of at most 0.0041.
Values may be sent and summed in bfloat16 or wider, within the bound.
No kernel may reach another device: no remote copies, remote signals or barrier semaphores. Data moves between devices by JAX's collectives and lax.ppermute only.
A program may use at most 64 MiB of HBM per device.

```python
import math
import jax
import jax.numpy as jnp
from jax import lax

NF = 36
ND = 36
LAT = 128
SUBSTEPS = 4
BINS = 1296
NBS = 8
SECTIONS = 4
NPTS = 4096


def draw_block_order(key, part):
    section_keys = jax.random.split(key, SECTIONS)
    orders = jax.vmap(lambda section_key: jax.random.permutation(section_key, NBS))(section_keys)
    return orders.reshape(-1).astype(jnp.int32)


def block_levels(stream_key, shape, cuts, least, top_value):
    gain, own = 1.0, jax.random.fold_in(stream_key, 6)
    for position, shards_of in cuts:
        heights = jnp.exp(jax.random.uniform(jax.random.fold_in(own, position), (shards_of,), jnp.float32, least / len(cuts), top_value / len(cuts)))
        gain = gain * jnp.repeat(heights, shape[position] // shards_of).reshape([-1 if axis == position else 1 for axis in range(len(shape))])
    return gain


def gaussian(key, dims, width, most, cuts=(), held_as=jnp.bfloat16):
    array = width * jax.random.normal(key, dims, jnp.float32)
    if cuts:
        array = array * block_levels(key, dims, cuts, -0.22, 0.18)
    return jnp.clip(array, -most, most).astype(held_as)


def setup_inputs(seed: int = 0) -> dict:
    arg_keys = jax.random.split(jax.random.key(seed), 5)
    return {
        "spectrum": jnp.clip(jnp.exp(math.log(2.0) - 2.9996462 * jax.random.uniform(arg_keys[0], (BINS, NPTS), jnp.float32) ** block_levels(arg_keys[0], (BINS, NPTS), ((1, 32),), -0.2, 0.2)), 0.099609375, 2.0).astype(jnp.bfloat16),
        "surface_wind": gaussian(arg_keys[1], (2, NPTS), 8.0, 30.0, ((1, 32),), jnp.float32),
        "wet_mask": jnp.clip(0.5 + 0.5 * jax.random.uniform(arg_keys[2], (NPTS,), jnp.float32) ** block_levels(arg_keys[2], (NPTS,), ((0, 32),), -0.2, 0.2), 0.5, 1.0),
        "block_order": draw_block_order(jax.random.fold_in(arg_keys[4], 71), 0),
    }


gravity = 9.81
base_freq = 0.035
freq_growth = 1.1
wind_rate = 0.015
dissip_rate = 0.008
steep_ref = 3.0
stress_coef = 0.01
courant = 0.62

def bin_tables(bin_index, freq_count, dir_count):
    total = freq_count * dir_count
    is_real = bin_index < total
    clamped = jnp.minimum(bin_index, total - 1)
    freq_pos = (clamped // dir_count).astype(jnp.float32)
    dir_pos = (clamped % dir_count).astype(jnp.float32)
    slowing = jnp.exp(-freq_pos * math.log(freq_growth))
    radian_freq = 2.0 * math.pi * base_freq / slowing
    wavenum = radian_freq * radian_freq / gravity
    phase_speed = gravity / radian_freq
    direction = dir_pos * (2.0 * math.pi / dir_count)
    dir_cos = jnp.cos(direction)
    dir_sin = jnp.sin(direction)
    bin_area = jnp.where(is_real, 0.1 * radian_freq * (2.0 * math.pi / dir_count), 0.0)
    travel = jnp.where(is_real, courant * slowing, 0.0)
    return (bin_area, radian_freq, wavenum, phase_speed, dir_cos, dir_sin, travel * dir_cos, travel * dir_sin)

def source_parts(spectra, wind_east, wind_north, tables):
    bin_area, radian_freq, wavenum, phase_speed, dir_cos, dir_sin = tables[:6]
    energy = spectra.astype(jnp.float32)
    weighted = bin_area[:, None] * energy
    moments = jnp.stack([lax.optimization_barrier(jnp.sum(weighted, axis=0)), lax.optimization_barrier(jnp.sum(weighted / radian_freq[:, None], axis=0)), lax.optimization_barrier(jnp.sum(weighted / jnp.sqrt(wavenum)[:, None], axis=0))])
    along = dir_cos[:, None] * wind_east[None, :] + dir_sin[:, None] * wind_north[None, :]
    growth = radian_freq[:, None] * jnp.maximum(0.0, 1.2 * along / phase_speed[:, None] - 1.0)
    flux_in = weighted * growth / phase_speed[:, None]
    momentum = jnp.stack([lax.optimization_barrier(jnp.sum(flux_in * dir_cos[:, None], axis=0)), lax.optimization_barrier(jnp.sum(flux_in * dir_sin[:, None], axis=0))])
    return (moments, growth, momentum)

def apply_sources(spectra, wetness, moments, growth, tables):
    wavenum = tables[2]
    mean_freq = moments[0] / moments[1]
    mean_wavenum = (moments[0] / moments[2]) ** 2
    steepness = moments[0] * mean_wavenum * mean_wavenum
    ratio = wavenum[:, None] / mean_wavenum[None, :]
    decay = (mean_freq * (steepness / steep_ref) ** 2)[None, :] * (0.5 * ratio + 0.5 * ratio * ratio)
    energy = spectra.astype(jnp.float32)
    return (wetness[None, :] * energy * jnp.exp(wind_rate * growth - dissip_rate * decay)).astype(jnp.bfloat16)

def advance(middle, from_west, from_east, speed_x, speed_y):
    lead = [(0, 0)] * (middle.ndim - 1)
    from_south = jnp.pad(middle[..., :-1], lead + [(1, 0)])
    from_north = jnp.pad(middle[..., 1:], lead + [(0, 1)])
    remain = 1.0 - jnp.abs(speed_x) - jnp.abs(speed_y)
    return remain * middle + jnp.maximum(speed_x, 0.0) * from_west + jnp.maximum(-speed_x, 0.0) * from_east + jnp.maximum(speed_y, 0.0) * from_south + jnp.maximum(-speed_y, 0.0) * from_north

def reference(spectrum, surface_wind, wet_mask, block_order):
    block_count = block_order.shape[0]
    slot_ids = jnp.arange(block_count, dtype=jnp.int32)
    grid_column = slot_ids // NBS * NBS + block_order
    inverse = jnp.zeros((block_count,), jnp.int32).at[grid_column].set(slot_ids)
    tables = bin_tables(jnp.arange(BINS, dtype=jnp.int32), NF, ND)
    wet_all = wet_mask

    def one_column(column_id):
        slot = inverse[column_id]
        spectra = lax.dynamic_slice_in_dim(spectrum, slot * LAT, LAT, 1)
        wind_here = lax.dynamic_slice_in_dim(surface_wind, column_id * LAT, LAT, 1)
        wetness = lax.dynamic_slice_in_dim(wet_all, column_id * LAT, LAT, 0)
        moments, growth, momentum = source_parts(spectra, wind_here[0], wind_here[1], tables)
        renewed = apply_sources(spectra, wetness, moments, growth, tables)
        return (renewed, wetness[None, :] * (stress_coef * momentum))
    renewed, stress = lax.map(one_column, slot_ids)
    renewed = lax.optimization_barrier(renewed)
    on_grid = jnp.transpose(renewed, (1, 0, 2))
    wet_grid = wet_all.reshape(block_count, LAT)

    def one_bin(operands):
        bin_plane, speed_x, speed_y = operands
        energy_field = bin_plane.astype(jnp.float32)
        for substep in range(SUBSTEPS):
            energy_field = wet_grid * advance(energy_field, jnp.roll(energy_field, 1, 0), jnp.roll(energy_field, -1, 0), speed_x, speed_y)
        return energy_field.astype(jnp.bfloat16)
    propagated = lax.map(one_bin, (on_grid, tables[6], tables[7]))
    new_spectrum = propagated[:, grid_column, :].reshape(BINS, block_count * LAT)
    wave_stress = jnp.transpose(stress, (1, 0, 2)).reshape(2, block_count * LAT)
    return (new_spectrum, wave_stress)
```

```python
import functools
import math

import jax
import jax.numpy as jnp
import numpy as np
from jax import lax
from jax.experimental import pallas as pl
from jax.experimental.pallas import tpu as pltpu
from jax.sharding import PartitionSpec as P

NF = 36
ND = 36
BINS = NF * ND
LAT = 128
SUBSTEPS = 4

gravity = 9.81
base_freq = 0.035
freq_growth = 1.1
wind_rate = 0.015
dissip_rate = 0.008
steep_ref = 3.0
stress_coef = 0.01
courant = 0.62

AXES = ("sec", "dom")
TILE = 8
GROUP_TILES = 9
BF = jnp.bfloat16
F32 = jnp.float32

FREQ = np.arange(NF, dtype=np.float64)
SIGMA = 2.0 * math.pi * base_freq * freq_growth**FREQ
WAVENUM = SIGMA * SIGMA / gravity
SPEED = gravity / SIGMA
AREA = 0.1 * SIGMA * (2.0 * math.pi / ND)
THETA = 2.0 * math.pi * np.arange(ND, dtype=np.float64) / ND
COS = np.cos(THETA)
SIN = np.sin(THETA)


def vmem():
    return pl.BlockSpec(memory_space=pltpu.VMEM)


def smem():
    return pl.BlockSpec(memory_space=pltpu.SMEM)


def layout(devices):
    each = BINS // devices
    rows = -(-(each + TILE) // 16) * 16
    return each, rows - TILE, rows


def device_tables(devices):
    each, kept, rows = layout(devices)
    table = np.zeros((devices, 8, rows), np.float64)
    for device in range(devices):
        bins = np.full((rows,), -1)
        bins[:each] = device * each + np.arange(each)
        if devices * each + device < BINS:
            bins[kept] = devices * each + device
        real = bins >= 0
        i, j = np.maximum(bins, 0) // ND, np.maximum(bins, 0) % ND
        scale = wind_rate * SIGMA[i]
        travel = courant * freq_growth ** (-i.astype(np.float64))
        cx, cy = travel * COS[j], travel * SIN[j]
        values = (
            scale * 1.2 / SPEED[i] * COS[j],
            scale * 1.2 / SPEED[i] * SIN[j],
            scale,
            1.0 - np.abs(cx) - np.abs(cy),
            np.maximum(cx, 0.0),
            np.maximum(-cx, 0.0),
            np.maximum(cy, 0.0),
            np.maximum(-cy, 0.0),
        )
        for row, value in enumerate(values):
            table[device, row] = np.where(real, value, 0.0)
    return table.astype(np.float32)


def split(value):
    high = value.astype(BF)
    return high.astype(F32), (value - high.astype(F32)).astype(BF).astype(F32)


def row_ids():
    return lax.broadcasted_iota(jnp.int32, (TILE, LAT), 0)


def stack_rows(rows):
    ids = row_ids()
    tile = jnp.zeros((TILE, LAT), F32)
    for r, row in enumerate(rows):
        if row is not None:
            tile = jnp.where(ids == r, jnp.broadcast_to(row, (TILE, LAT)), tile)
    return tile


def tile_freqs(t):
    return (TILE * t) // ND, (TILE * t + TILE - 1) // ND


def decayed_tiles(spectrum_ref):
    ids = row_ids()
    upper = ids < TILE // 2
    tiles = []
    for pair in range(BINS // 16):
        both = spectrum_ref[16 * pair : 16 * pair + 16, :].astype(F32)
        tiles += [both[:TILE], both[TILE:]]
    sums = [jnp.zeros((TILE, LAT), F32) for _ in range(3)]
    for group in range(NF // 2):
        nine = tiles[GROUP_TILES * group : GROUP_TILES * (group + 1)]
        low = (nine[0] + nine[1]) + (nine[2] + nine[3]) + jnp.where(upper, nine[4], 0.0)
        high = (nine[5] + nine[6]) + (nine[7] + nine[8]) + jnp.where(upper, 0.0, nine[4])
        for i, part in ((2 * group, low), (2 * group + 1, high)):
            weights = (AREA[i], AREA[i] / SIGMA[i], AREA[i] / math.sqrt(WAVENUM[i]))
            sums = [s + float(np.float32(w)) * part for s, w in zip(sums, weights)]
    moments = [jnp.broadcast_to(jnp.sum(s, axis=0, keepdims=True), (TILE, LAT)) for s in sums]
    mean_freq = moments[0] / moments[1]
    mean_wavenum = (moments[0] / moments[2]) ** 2
    steepness = moments[0] * mean_wavenum * mean_wavenum
    strength = mean_freq * (steepness / steep_ref) ** 2
    inverse = 1.0 / mean_wavenum
    factors = []
    for i in range(NF):
        ratio = float(np.float32(WAVENUM[i])) * inverse
        factors.append(jnp.exp(-dissip_rate * (strength * (0.5 * ratio + 0.5 * ratio * ratio))))
    out = []
    for t, tile in enumerate(tiles):
        first, last = tile_freqs(t)
        factor = factors[first]
        if last != first:
            factor = jnp.where(upper, factor, factors[last])
        out.append(tile * factor)
    return out


def shared_tile(wind_ref, wet_ref, order):
    east, north, wet = split(wind_ref[0:1, :]), split(wind_ref[1:2, :]), split(wet_ref[0:1, :])
    column = jnp.full((1, LAT), order, jnp.int32).astype(F32)
    return stack_rows([None, *east, *north, *wet, column])


def pack_kernel(devices, order_ref, spectrum_ref, wind_ref, wet_ref, out_ref):
    each, kept, rows = layout(devices)
    tiles = decayed_tiles(spectrum_ref)
    shared = shared_tile(wind_ref, wet_ref, order_ref[0])
    first = row_ids() == 0
    left = BINS - devices * each
    per = each // TILE
    for d in range(devices):
        last = shared
        if d < left:
            spare = tiles[per * devices + d // TILE]
            row = spare[d % TILE : d % TILE + 1]
            last = jnp.where(first, jnp.broadcast_to(row, (TILE, LAT)), shared)
        chunk = jnp.concatenate(tiles[per * d : per * (d + 1)] + [last], axis=0)
        out_ref[d] = chunk.astype(BF)


def loose_kernel(order_ref, spectrum_ref, wind_ref, wet_ref, out_ref, shared_ref):
    tiles = decayed_tiles(spectrum_ref)
    for pair in range(BINS // 16):
        both = jnp.concatenate(tiles[2 * pair : 2 * pair + 2], axis=0)
        out_ref[16 * pair : 16 * pair + 16, :] = both.astype(BF)
    shared_ref[...] = shared_tile(wind_ref, wet_ref, order_ref[0])


def packed(devices, block_order, spectrum, surface_wind, wet):
    each, kept, rows = layout(devices)
    shape = jax.ShapeDtypeStruct((devices, rows, LAT), BF)
    params = pltpu.CompilerParams(vmem_limit_bytes=24 << 20)
    in_specs = [smem(), vmem(), vmem(), vmem()]
    if each == kept:
        return pl.pallas_call(
            functools.partial(pack_kernel, devices),
            out_shape=shape,
            in_specs=in_specs,
            out_specs=vmem(),
            compiler_params=params,
        )(block_order, spectrum, surface_wind, wet)
    decayed, shared = pl.pallas_call(
        loose_kernel,
        out_shape=(
            jax.ShapeDtypeStruct((BINS, LAT), BF),
            jax.ShapeDtypeStruct((TILE, LAT), F32),
        ),
        in_specs=in_specs,
        out_specs=(vmem(), vmem()),
        compiler_params=params,
    )(block_order, spectrum, surface_wind, wet)
    main = decayed[: devices * each].reshape(devices, each, LAT)
    main = jnp.pad(main, ((0, 0), (0, kept - each), (0, 0)))
    spare = decayed[devices * each :]
    spare = jnp.pad(spare, ((0, devices - spare.shape[0]), (0, 0)))[:, None]
    common = jnp.broadcast_to(shared[1:].astype(BF)[None], (devices, TILE - 1, LAT))
    return jnp.concatenate([main, spare, common], axis=1)


def own_stress(spectrum_ref, angles_ref, east, north):
    upper = row_ids() < TILE // 2
    cosines = [angles_ref[0, TILE * p : TILE * (p + 1), :] for p in range(GROUP_TILES)]
    sines = [angles_ref[1, TILE * p : TILE * (p + 1), :] for p in range(GROUP_TILES)]
    along = [c * east + s * north for c, s in zip(cosines, sines)]
    totals = [jnp.zeros((TILE, LAT), F32) for _ in range(GROUP_TILES)]

    def constant(values, first, last):
        low, high = float(np.float32(values[first])), float(np.float32(values[last]))
        return low if first == last else jnp.where(upper, low, high)

    for pair in range(BINS // 16):
        both = spectrum_ref[16 * pair : 16 * pair + 16, :].astype(F32)
        for half in range(2):
            t = 2 * pair + half
            p = t % GROUP_TILES
            tile = both[TILE * half : TILE * (half + 1)]
            slope = constant(1.2 / SPEED, *tile_freqs(t))
            weight = constant(stress_coef * AREA * SIGMA / SPEED, *tile_freqs(t))
            grown = jnp.maximum(0.0, slope * along[p] - 1.0)
            totals[p] = totals[p] + (weight * tile) * grown
    return [
        jnp.sum(sum(a * b for a, b in zip(parts, totals)), axis=0, keepdims=True)
        for parts in (cosines, sines)
    ]


def spread_kernel(
    devices, section, order_ref, recv_ref, spectrum_ref, table_ref, angles_ref, out_ref,
    field_a, field_b, wet_ref, order_vmem, order_smem, column_smem, slot_smem, sem,
):
    each, kept, rows = layout(devices)
    ids = row_ids()
    lane = lax.broadcasted_iota(jnp.int32, (TILE, LAT), 1)
    blocks = -(-devices // LAT)
    for block in range(blocks):

        def place(s, tile, block=block):
            here = recv_ref[block * LAT + s, kept : kept + TILE, :].astype(F32)
            return jnp.where(lane == s, here, tile)

        count = min(LAT, devices - block * LAT)
        orders = lax.fori_loop(0, count, place, jnp.zeros((TILE, LAT), F32), unroll=8)
        order_vmem[block] = orders.astype(jnp.int32)
    copy = pltpu.make_async_copy(order_vmem, order_smem, sem)
    copy.start()
    copy.wait()

    def number(s, carry):
        column = s // section * section + order_smem[s // LAT, TILE - 1, s % LAT]
        column_smem[s] = column
        slot_smem[column] = s
        return carry

    lax.fori_loop(0, devices, number, 0, unroll=8)

    def weather(column):
        tile = recv_ref[column, kept : kept + TILE, :].astype(F32)
        east, north = tile[1:2] + tile[2:3], tile[3:4] + tile[4:5]
        return east, north, tile[5:6] + tile[6:7]

    me = lax.axis_index("sec") * section + lax.axis_index("dom")
    stress = own_stress(spectrum_ref, angles_ref, *weather(me // section * section + order_ref[0])[:2])
    parts = split(stress[0]) + split(stress[1])
    column_row = jnp.full((1, LAT), order_ref[0], jnp.int32).astype(F32)
    ending = stack_rows([None, *parts, None, None, column_row])

    def renew(column, carry):
        east, north, wet = weather(column)
        wet_ref[column] = jnp.broadcast_to(wet, (TILE, LAT))
        energy = recv_ref[slot_smem[column]].astype(F32)
        push = jnp.exp(
            jnp.maximum(0.0, table_ref[0] * east + table_ref[1] * north - table_ref[2])
        )
        field_a[column] = (wet * energy * push).astype(BF).astype(F32)
        return carry

    lax.fori_loop(0, devices, renew, 0, unroll=2)

    def moved(source, column):
        here = source[column]
        west = source[jnp.where(column == 0, devices - 1, column - 1)]
        east = source[jnp.where(column == devices - 1, 0, column + 1)]
        total = table_ref[3] * here + table_ref[4] * west + table_ref[5] * east
        total = total + table_ref[6] * pltpu.roll(here, 1, 1)
        total = total + table_ref[7] * pltpu.roll(here, LAT - 1, 1)
        return wet_ref[column, 0:1, :] * total

    fields = (field_a, field_b)
    for substep in range(SUBSTEPS - 1):
        source, target = fields[substep % 2], fields[(substep + 1) % 2]

        def step(column, carry, source=source, target=target):
            target[column] = moved(source, column)
            return carry

        lax.fori_loop(0, devices, step, 0, unroll=2)
    source = fields[(SUBSTEPS - 1) % 2]

    def finish(column, carry):
        total = moved(source, column)
        last = jnp.where(ids == 0, total[kept:], ending)
        out_ref[slot_smem[column]] = jnp.concatenate([total[:kept], last], axis=0).astype(BF)
        return carry

    lax.fori_loop(0, devices, finish, 0, unroll=2)


def spread(devices, section, block_order, received, spectrum, table):
    each, kept, rows = layout(devices)
    angle = np.arange(GROUP_TILES * TILE) % ND
    angles = np.broadcast_to(
        np.stack([COS[angle], SIN[angle]]).astype(np.float32)[:, :, None],
        (2, GROUP_TILES * TILE, LAT),
    )
    blocks = -(-devices // LAT)
    return pl.pallas_call(
        functools.partial(spread_kernel, devices, section),
        out_shape=jax.ShapeDtypeStruct((devices, rows, LAT), BF),
        in_specs=[smem(), vmem(), vmem(), vmem(), vmem()],
        out_specs=vmem(),
        scratch_shapes=[
            pltpu.VMEM((devices, rows, LAT), F32),
            pltpu.VMEM((devices, rows, LAT), F32),
            pltpu.VMEM((devices, TILE, LAT), F32),
            pltpu.VMEM((blocks, TILE, LAT), jnp.int32),
            pltpu.SMEM((blocks, TILE, LAT), jnp.int32),
            pltpu.SMEM((devices,), jnp.int32),
            pltpu.SMEM((devices,), jnp.int32),
            pltpu.SemaphoreType.DMA,
        ],
        compiler_params=pltpu.CompilerParams(vmem_limit_bytes=32 << 20),
    )(block_order, received, spectrum, table, jnp.asarray(angles))


def collect(devices, section, returned_ref, wet_ref, stress_ref):
    each, kept, rows = layout(devices)
    base = lax.axis_index("sec") * section
    rank = lax.axis_index("dom").astype(F32)

    def pick(s, total):
        tile = returned_ref[base + s, kept : kept + TILE, :].astype(F32)
        mine = jnp.broadcast_to(tile[TILE - 1 : TILE] == rank, (TILE, LAT))
        return jnp.where(mine, tile, total)

    tile = lax.fori_loop(0, section, pick, jnp.zeros((TILE, LAT), F32), unroll=8)
    wet = wet_ref[0:1, :]
    stress_ref[0:1, :] = wet * (tile[1:2] + tile[2:3])
    stress_ref[1:2, :] = wet * (tile[3:4] + tile[4:5])


def unpack_kernel(devices, section, returned_ref, wet_ref, out_ref, stress_ref):
    each, kept, rows = layout(devices)
    left = BINS - devices * each
    for pair in range(devices // 2):
        both = [returned_ref[2 * pair + half].astype(F32)[:each] for half in range(2)]
        out_ref[2 * each * pair : 2 * each * (pair + 1), :] = jnp.concatenate(both, axis=0).astype(BF)
    spare = []
    for tile in range(left // TILE):
        heads = [returned_ref[TILE * tile + r].astype(F32)[kept : kept + 1] for r in range(TILE)]
        spare.append(stack_rows(heads))
    out_ref[devices * each :, :] = jnp.concatenate(spare, axis=0).astype(BF)
    collect(devices, section, returned_ref, wet_ref, stress_ref)


def unpacked(devices, section, returned, wet):
    each, kept, rows = layout(devices)
    left = BINS - devices * each
    stress_shape = jax.ShapeDtypeStruct((2, LAT), F32)
    params = pltpu.CompilerParams(vmem_limit_bytes=24 << 20)
    if each == kept and devices % 2 == 0 and each % TILE == 0 and left % 16 == 0:
        return pl.pallas_call(
            functools.partial(unpack_kernel, devices, section),
            out_shape=(jax.ShapeDtypeStruct((BINS, LAT), BF), stress_shape),
            in_specs=[vmem(), vmem()],
            out_specs=(vmem(), vmem()),
            compiler_params=params,
        )(returned, wet)
    stress = pl.pallas_call(
        functools.partial(collect, devices, section),
        out_shape=stress_shape,
        in_specs=[vmem(), vmem()],
        out_specs=vmem(),
        compiler_params=params,
    )(returned, wet)
    main = returned[:, :each].reshape(devices * each, LAT)
    return jnp.concatenate([main, returned[:left, kept]], axis=0), stress


def on_device(devices, section, spectrum, surface_wind, wet_mask, block_order):
    wet = wet_mask.reshape(1, LAT)
    each, kept, rows = layout(devices)
    me = lax.axis_index(AXES)
    numbers = lax.dynamic_index_in_dim(jnp.asarray(device_tables(devices)), me, 0, keepdims=False)
    table = jnp.broadcast_to(numbers[:, :, None], (8, rows, LAT))
    lat = jnp.arange(LAT)
    which = jnp.arange(8)[:, None, None]
    edge = ((which == 6) & (lat == 0)) | ((which == 7) & (lat == LAT - 1))
    table = jnp.where(edge, 0.0, table)
    sending = packed(devices, block_order, spectrum, surface_wind, wet)
    received = lax.all_to_all(sending, AXES, split_axis=0, concat_axis=0, tiled=True)
    leaving = spread(devices, section, block_order, received, spectrum, table)
    returned = lax.all_to_all(leaving, AXES, split_axis=0, concat_axis=0, tiled=True)
    return unpacked(devices, section, returned, wet)


def solution(mesh):
    section = mesh.shape["dom"]
    devices = mesh.shape["sec"] * section
    placed = (P(None, AXES), P(None, AXES), P(AXES), P(AXES))
    return jax.shard_map(
        functools.partial(on_device, devices, section),
        mesh=mesh,
        in_specs=placed,
        out_specs=(P(None, AXES), P(None, AXES)),
        check_vma=False,
    )
```

```python
import functools
import math

import jax
import jax.numpy as jnp
import numpy as np
from jax import lax
from jax.experimental import pallas as pl
from jax.experimental.pallas import tpu as pltpu
from jax.sharding import PartitionSpec as P

NF = 36
ND = 36
BINS = NF * ND
LAT = 128
SUBSTEPS = 4

gravity = 9.81
base_freq = 0.035
freq_growth = 1.1
wind_rate = 0.015
dissip_rate = 0.008
steep_ref = 3.0
stress_coef = 0.01
courant = 0.62

AXES = ("sec", "dom")
TILE = 8
UNROLL = 32
GROUP_TILES = 9
BF = jnp.bfloat16
F32 = jnp.float32

FREQ = np.arange(NF, dtype=np.float64)
SIGMA = 2.0 * math.pi * base_freq * freq_growth**FREQ
WAVENUM = SIGMA * SIGMA / gravity
SPEED = gravity / SIGMA
AREA = 0.1 * SIGMA * (2.0 * math.pi / ND)
THETA = 2.0 * math.pi * np.arange(ND, dtype=np.float64) / ND
COS = np.cos(THETA)
SIN = np.sin(THETA)


def vmem():
    return pl.BlockSpec(memory_space=pltpu.VMEM)


def smem():
    return pl.BlockSpec(memory_space=pltpu.SMEM)


def layout(devices):
    each = BINS // devices
    rows = -(-(each + TILE) // 16) * 16
    return each, rows - TILE, rows


def device_tables(devices):
    each, kept, rows = layout(devices)
    table = np.zeros((devices, 8, rows), np.float64)
    for device in range(devices):
        bins = np.full((rows,), -1)
        bins[:each] = device * each + np.arange(each)
        if devices * each + device < BINS:
            bins[kept] = devices * each + device
        real = bins >= 0
        i, j = np.maximum(bins, 0) // ND, np.maximum(bins, 0) % ND
        scale = wind_rate * SIGMA[i]
        travel = courant * freq_growth ** (-i.astype(np.float64))
        cx, cy = travel * COS[j], travel * SIN[j]
        values = (
            scale * 1.2 / SPEED[i] * COS[j],
            scale * 1.2 / SPEED[i] * SIN[j],
            scale,
            1.0 - np.abs(cx) - np.abs(cy),
            np.maximum(cx, 0.0),
            np.maximum(-cx, 0.0),
            np.maximum(cy, 0.0),
            np.maximum(-cy, 0.0),
        )
        for row, value in enumerate(values):
            table[device, row] = np.where(real, value, 0.0)
    angle = np.arange(GROUP_TILES * TILE) % ND
    angles = np.concatenate([COS[angle], SIN[angle]])
    angles = np.broadcast_to(angles, (devices, angles.size))
    return np.concatenate([table.reshape(devices, -1), angles], axis=1).astype(np.float32)


def own_table(devices, me):
    starts = table_rows(devices)[0] + [8 * layout(devices)[2]]
    numbers = lax.dynamic_index_in_dim(jnp.asarray(device_tables(devices)), me, 0, keepdims=False)
    row, lat = jnp.arange(numbers.shape[0])[:, None], jnp.arange(LAT)[None, :]
    south = (row >= starts[6]) & (row < starts[7]) & (lat == 0)
    north = (row >= starts[7]) & (row < starts[8]) & (lat == LAT - 1)
    return jnp.where(south | north, 0.0, jnp.broadcast_to(numbers[:, None], (numbers.shape[0], LAT)))


def split(value):
    high = value.astype(BF)
    return high.astype(F32), (value - high.astype(F32)).astype(BF).astype(F32)


def row_ids():
    return lax.broadcasted_iota(jnp.int32, (TILE, LAT), 0)


def stack_rows(rows):
    ids = row_ids()
    tile = jnp.zeros((TILE, LAT), F32)
    for r, row in enumerate(rows):
        if row is not None:
            tile = jnp.where(ids == r, jnp.broadcast_to(row, (TILE, LAT)), tile)
    return tile


def tile_freqs(t):
    return (TILE * t) // ND, (TILE * t + TILE - 1) // ND


def decayed_tiles(spectrum_ref):
    ids = row_ids()
    upper = ids < TILE // 2
    tiles = []
    for pair in range(BINS // 16):
        both = spectrum_ref[16 * pair : 16 * pair + 16, :].astype(F32)
        tiles += [both[:TILE], both[TILE:]]
    sums = [jnp.zeros((TILE, LAT), F32) for _ in range(3)]
    for group in range(NF // 2):
        nine = tiles[GROUP_TILES * group : GROUP_TILES * (group + 1)]
        low = (nine[0] + nine[1]) + (nine[2] + nine[3]) + jnp.where(upper, nine[4], 0.0)
        high = (nine[5] + nine[6]) + (nine[7] + nine[8]) + jnp.where(upper, 0.0, nine[4])
        for i, part in ((2 * group, low), (2 * group + 1, high)):
            weights = (AREA[i], AREA[i] / SIGMA[i], AREA[i] / math.sqrt(WAVENUM[i]))
            sums = [s + float(np.float32(w)) * part for s, w in zip(sums, weights)]
    moments = [jnp.broadcast_to(jnp.sum(s, axis=0, keepdims=True), (TILE, LAT)) for s in sums]
    mean_freq = moments[0] / moments[1]
    mean_wavenum = (moments[0] / moments[2]) ** 2
    steepness = moments[0] * mean_wavenum * mean_wavenum
    strength = mean_freq * (steepness / steep_ref) ** 2
    inverse = 1.0 / mean_wavenum
    factors = []
    for i in range(NF):
        ratio = float(np.float32(WAVENUM[i])) * inverse
        factors.append(jnp.exp(-dissip_rate * (strength * (0.5 * ratio + 0.5 * ratio * ratio))))
    out = []
    for t, tile in enumerate(tiles):
        first, last = tile_freqs(t)
        factor = factors[first]
        if last != first:
            factor = jnp.where(upper, factor, factors[last])
        out.append(tile * factor)
    return out


def shared_tile(wind_ref, wet_ref, order):
    east, north, wet = split(wind_ref[0:1, :]), split(wind_ref[1:2, :]), split(wet_ref[0:1, :])
    column = jnp.full((1, LAT), order, jnp.int32).astype(F32)
    return stack_rows([None, *east, *north, *wet, column])


def pack_kernel(devices, order_ref, spectrum_ref, wind_ref, wet_ref, out_ref):
    each, kept, rows = layout(devices)
    tiles = decayed_tiles(spectrum_ref)
    shared = shared_tile(wind_ref, wet_ref, order_ref[0])
    first = row_ids() == 0
    left = BINS - devices * each
    per = each // TILE
    for d in range(devices):
        last = shared
        if d < left:
            spare = tiles[per * devices + d // TILE]
            row = spare[d % TILE : d % TILE + 1]
            last = jnp.where(first, jnp.broadcast_to(row, (TILE, LAT)), shared)
        chunk = jnp.concatenate(tiles[per * d : per * (d + 1)] + [last], axis=0)
        out_ref[d] = chunk.astype(BF)


def loose_kernel(order_ref, spectrum_ref, wind_ref, wet_ref, out_ref, shared_ref):
    tiles = decayed_tiles(spectrum_ref)
    for pair in range(BINS // 16):
        both = jnp.concatenate(tiles[2 * pair : 2 * pair + 2], axis=0)
        out_ref[16 * pair : 16 * pair + 16, :] = both.astype(BF)
    shared_ref[...] = shared_tile(wind_ref, wet_ref, order_ref[0])


def packed(devices, block_order, spectrum, surface_wind, wet):
    each, kept, rows = layout(devices)
    shape = jax.ShapeDtypeStruct((devices, rows, LAT), BF)
    params = pltpu.CompilerParams(vmem_limit_bytes=24 << 20)
    in_specs = [smem(), vmem(), vmem(), vmem()]
    if each == kept:
        return pl.pallas_call(
            functools.partial(pack_kernel, devices),
            out_shape=shape,
            in_specs=in_specs,
            out_specs=vmem(),
            compiler_params=params,
        )(block_order, spectrum, surface_wind, wet)
    decayed, shared = pl.pallas_call(
        loose_kernel,
        out_shape=(
            jax.ShapeDtypeStruct((BINS, LAT), BF),
            jax.ShapeDtypeStruct((TILE, LAT), F32),
        ),
        in_specs=in_specs,
        out_specs=(vmem(), vmem()),
        compiler_params=params,
    )(block_order, spectrum, surface_wind, wet)
    main = decayed[: devices * each].reshape(devices, each, LAT)
    main = jnp.pad(main, ((0, 0), (0, kept - each), (0, 0)))
    spare = decayed[devices * each :]
    spare = jnp.pad(spare, ((0, devices - spare.shape[0]), (0, 0)))[:, None]
    common = jnp.broadcast_to(shared[1:].astype(BF)[None], (devices, TILE - 1, LAT))
    return jnp.concatenate([main, spare, common], axis=1)


def own_stress(spectrum_ref, cosine, sine, east, north):
    upper = row_ids() < TILE // 2
    cosines = [cosine[TILE * p : TILE * (p + 1)] for p in range(GROUP_TILES)]
    sines = [sine[TILE * p : TILE * (p + 1)] for p in range(GROUP_TILES)]
    along = [c * east + s * north for c, s in zip(cosines, sines)]
    totals = [jnp.zeros((TILE, LAT), F32) for _ in range(GROUP_TILES)]

    def constant(values, first, last):
        low, high = float(np.float32(values[first])), float(np.float32(values[last]))
        return low if first == last else jnp.where(upper, low, high)

    for pair in range(BINS // 16):
        both = spectrum_ref[16 * pair : 16 * pair + 16, :].astype(F32)
        for half in range(2):
            t = 2 * pair + half
            p = t % GROUP_TILES
            tile = both[TILE * half : TILE * (half + 1)]
            slope = constant(1.2 / SPEED, *tile_freqs(t))
            weight = constant(stress_coef * AREA * SIGMA / SPEED, *tile_freqs(t))
            grown = jnp.maximum(0.0, slope * along[p] - 1.0)
            totals[p] = totals[p] + (weight * tile) * grown
    return [
        jnp.sum(sum(a * b for a, b in zip(parts, totals)), axis=0, keepdims=True)
        for parts in (cosines, sines)
    ]


def table_rows(devices):
    rows = layout(devices)[2]
    return [k * rows for k in range(8)], [8 * rows + k * GROUP_TILES * TILE for k in range(2)]


def spread_kernel(
    devices, section, order_ref, recv_ref, spectrum_ref, table_ref, out_ref,
    field_a, field_b, wet_ref, order_vmem, order_smem, slot_smem, sem,
):
    each, kept, rows = layout(devices)
    starts, angle_starts = table_rows(devices)
    ids = row_ids()
    lane = lax.broadcasted_iota(jnp.int32, (TILE, LAT), 1)
    unit = math.gcd(devices, UNROLL)

    def every(body):
        if devices == unit:
            for column in range(devices):
                body(column)
            return

        def some(block, carry):
            for k in range(unit):
                body(block * unit + k)
            return carry

        lax.fori_loop(0, devices // unit, some, 0)

    span = min(LAT, devices)
    for block in range(devices // span):

        def place(s, tile, block=block):
            here = recv_ref[block * span + s, kept : kept + TILE, :].astype(F32)
            return jnp.where(lane == s, here, tile)

        orders = lax.fori_loop(0, span, place, jnp.zeros((TILE, LAT), F32), unroll=min(span, UNROLL))
        order_vmem[block] = orders.astype(jnp.int32)
    copy = pltpu.make_async_copy(order_vmem, order_smem, sem)
    copy.start()
    copy.wait()

    def number(s):
        column = s // section * section + order_smem[s // span, TILE - 1, s % span]
        slot_smem[column] = s

    every(number)

    def weather(column):
        tile = recv_ref[column, kept : kept + TILE, :].astype(F32)
        return tile[1:2] + tile[2:3], tile[3:4] + tile[4:5], tile[5:6] + tile[6:7]

    base = lax.axis_index("sec") * section
    angles = [table_ref[pl.ds(start, GROUP_TILES * TILE), :] for start in angle_starts]
    stress = own_stress(spectrum_ref, *angles, *weather(base + order_ref[0])[:2])
    column_row = jnp.full((1, LAT), order_ref[0], jnp.int32).astype(F32)
    ending = stack_rows([None, *split(stress[0]), *split(stress[1]), None, None, column_row])

    def numbers(k, first=0, count=rows):
        return table_ref[pl.ds(starts[k] + first, count), :]

    def renew(column):
        east, north, wet = weather(column)
        wet_ref[column] = jnp.broadcast_to(wet, (TILE, LAT))
        energy = recv_ref[slot_smem[column]].astype(F32)
        push = jnp.exp(jnp.maximum(0.0, numbers(0) * east + numbers(1) * north - numbers(2)))
        field_a[column] = wet * energy * push

    every(renew)

    for substep in range(SUBSTEPS):
        source, target = (field_a, field_b) if substep % 2 == 0 else (field_b, field_a)
        for t in range(rows // TILE):
            part = pl.ds(TILE * t, TILE)
            keep, from_west, from_east, from_south, from_north = (
                numbers(k, TILE * t, TILE) for k in range(3, 8)
            )

            def step(column):
                if isinstance(column, int):
                    west, east = (column - 1) % devices, (column + 1) % devices
                else:
                    west = jnp.where(column == 0, devices - 1, column - 1)
                    east = jnp.where(column == devices - 1, 0, column + 1)
                here = source[column, part, :]
                total = keep * here + from_west * source[west, part, :]
                total = total + from_east * source[east, part, :]
                total = total + from_south * pltpu.roll(here, 1, 1)
                total = total + from_north * pltpu.roll(here, LAT - 1, 1)
                target[column, part, :] = wet_ref[column] * total

            every(step)

    final = field_a if SUBSTEPS % 2 == 0 else field_b

    def finish(column):
        last = jnp.where(ids == 0, final[column, kept:, :], ending)
        whole = jnp.concatenate([final[column, :kept, :], last], axis=0)
        out_ref[slot_smem[column]] = whole.astype(BF)

    every(finish)


def spread(devices, section, block_order, received, spectrum, table):
    each, kept, rows = layout(devices)
    span = min(LAT, devices)
    return pl.pallas_call(
        functools.partial(spread_kernel, devices, section),
        out_shape=jax.ShapeDtypeStruct((devices, rows, LAT), BF),
        in_specs=[smem(), vmem(), vmem(), vmem()],
        out_specs=vmem(),
        scratch_shapes=[
            pltpu.VMEM((devices, rows, LAT), F32),
            pltpu.VMEM((devices, rows, LAT), F32),
            pltpu.VMEM((devices, TILE, LAT), F32),
            pltpu.VMEM((devices // span, TILE, LAT), jnp.int32),
            pltpu.SMEM((devices // span, TILE, LAT), jnp.int32),
            pltpu.SMEM((devices,), jnp.int32),
            pltpu.SemaphoreType.DMA,
        ],
        compiler_params=pltpu.CompilerParams(vmem_limit_bytes=32 << 20),
    )(block_order, received, spectrum, table)


def collect(devices, section, returned_ref, wet_ref, stress_ref):
    each, kept, rows = layout(devices)
    base = lax.axis_index("sec") * section
    rank = lax.axis_index("dom").astype(F32)

    def pick(s, total):
        tile = returned_ref[base + s, kept : kept + TILE, :].astype(F32)
        mine = jnp.broadcast_to(tile[TILE - 1 : TILE] == rank, (TILE, LAT))
        return jnp.where(mine, tile, total)

    tile = lax.fori_loop(0, section, pick, jnp.zeros((TILE, LAT), F32), unroll=8)
    wet = wet_ref[0:1, :]
    stress_ref[0:1, :] = wet * (tile[1:2] + tile[2:3])
    stress_ref[1:2, :] = wet * (tile[3:4] + tile[4:5])


def unpack_kernel(devices, section, returned_ref, wet_ref, out_ref, stress_ref):
    each, kept, rows = layout(devices)
    left = BINS - devices * each
    for pair in range(devices // 2):
        both = [returned_ref[2 * pair + half].astype(F32)[:each] for half in range(2)]
        out_ref[2 * each * pair : 2 * each * (pair + 1), :] = jnp.concatenate(both, axis=0).astype(BF)
    spare = []
    for tile in range(left // TILE):
        heads = [returned_ref[TILE * tile + r].astype(F32)[kept : kept + 1] for r in range(TILE)]
        spare.append(stack_rows(heads))
    out_ref[devices * each :, :] = jnp.concatenate(spare, axis=0).astype(BF)
    collect(devices, section, returned_ref, wet_ref, stress_ref)


def unpacked(devices, section, returned, wet):
    each, kept, rows = layout(devices)
    left = BINS - devices * each
    stress_shape = jax.ShapeDtypeStruct((2, LAT), F32)
    params = pltpu.CompilerParams(vmem_limit_bytes=24 << 20)
    if each == kept and devices % 2 == 0 and each % TILE == 0 and left % 16 == 0:
        return pl.pallas_call(
            functools.partial(unpack_kernel, devices, section),
            out_shape=(jax.ShapeDtypeStruct((BINS, LAT), BF), stress_shape),
            in_specs=[vmem(), vmem()],
            out_specs=(vmem(), vmem()),
            compiler_params=params,
        )(returned, wet)
    stress = pl.pallas_call(
        functools.partial(collect, devices, section),
        out_shape=stress_shape,
        in_specs=[vmem(), vmem()],
        out_specs=vmem(),
        compiler_params=params,
    )(returned, wet)
    main = returned[:, :each].reshape(devices * each, LAT)
    return jnp.concatenate([main, returned[:left, kept]], axis=0), stress


def on_device(devices, section, spectrum, surface_wind, wet_mask, block_order):
    wet = wet_mask.reshape(1, LAT)
    each, kept, rows = layout(devices)
    table = own_table(devices, lax.axis_index(AXES))
    sending = packed(devices, block_order, spectrum, surface_wind, wet)
    received = lax.all_to_all(sending, AXES, split_axis=0, concat_axis=0, tiled=True)
    leaving = spread(devices, section, block_order, received, spectrum, table)
    returned = lax.all_to_all(leaving, AXES, split_axis=0, concat_axis=0, tiled=True)
    return unpacked(devices, section, returned, wet)


def solution(mesh):
    section = mesh.shape["dom"]
    devices = mesh.shape["sec"] * section
    placed = (P(None, AXES), P(None, AXES), P(AXES), P(AXES))
    return jax.shard_map(
        functools.partial(on_device, devices, section),
        mesh=mesh,
        in_specs=placed,
        out_specs=(P(None, AXES), P(None, AXES)),
        check_vma=False,
    )
```

```python
import functools
import math

import jax
import jax.numpy as jnp
import numpy as np
from jax import lax
from jax.experimental import pallas as pl
from jax.experimental.pallas import tpu as pltpu
from jax.sharding import PartitionSpec as P

NF = 36
ND = 36
BINS = NF * ND
LAT = 128
SUBSTEPS = 4

gravity = 9.81
base_freq = 0.035
freq_growth = 1.1
wind_rate = 0.015
dissip_rate = 0.008
steep_ref = 3.0
stress_coef = 0.01
courant = 0.62

AXES = ("sec", "dom")
TILE = 8
UNROLL = 32
PART = 144
PARTS = BINS // PART
LEAVING = 4
GROUP_TILES = 9
BF = jnp.bfloat16
F32 = jnp.float32

FREQ = np.arange(NF, dtype=np.float64)
SIGMA = 2.0 * math.pi * base_freq * freq_growth**FREQ
WAVENUM = SIGMA * SIGMA / gravity
SPEED = gravity / SIGMA
AREA = 0.1 * SIGMA * (2.0 * math.pi / ND)
THETA = 2.0 * math.pi * np.arange(ND, dtype=np.float64) / ND
COS = np.cos(THETA)
SIN = np.sin(THETA)


def vmem():
    return pl.BlockSpec(memory_space=pltpu.VMEM)


def smem():
    return pl.BlockSpec(memory_space=pltpu.SMEM)


def anywhere():
    return pl.BlockSpec(memory_space=pl.ANY)


def layout(devices):
    each = BINS // devices
    rows = -(-(each + TILE) // 16) * 16
    return each, rows - TILE, rows


def device_tables(devices):
    each, kept, rows = layout(devices)
    table = np.zeros((devices, rows, LAT), np.float64)
    for device in range(devices):
        bins = np.full((rows,), -1)
        bins[:each] = device * each + np.arange(each)
        if devices * each + device < BINS:
            bins[kept] = devices * each + device
        real = bins >= 0
        i, j = np.maximum(bins, 0) // ND, np.maximum(bins, 0) % ND
        scale = wind_rate * SIGMA[i]
        travel = courant * freq_growth ** (-i.astype(np.float64))
        cx, cy = travel * COS[j], travel * SIN[j]
        values = (
            scale * 1.2 / SPEED[i] * COS[j],
            scale * 1.2 / SPEED[i] * SIN[j],
            scale,
            1.0 - np.abs(cx) - np.abs(cy),
            np.maximum(cx, 0.0),
            np.maximum(-cx, 0.0),
            np.maximum(cy, 0.0),
            np.maximum(-cy, 0.0),
        )
        for lane, value in enumerate(values):
            table[device, :, lane] = np.where(real, value, 0.0)
    return table.astype(np.float32)


def angle_table():
    table = np.zeros((GROUP_TILES * TILE, LAT), np.float64)
    angle = np.arange(GROUP_TILES * TILE) % ND
    table[:, 0], table[:, 1] = COS[angle], SIN[angle]
    return table.astype(np.float32)


def split(value):
    high = value.astype(BF)
    return high.astype(F32), (value - high.astype(F32)).astype(BF).astype(F32)


def row_ids():
    return lax.broadcasted_iota(jnp.int32, (TILE, LAT), 0)


def stack_rows(rows):
    ids = row_ids()
    tile = jnp.zeros((TILE, LAT), F32)
    for r, row in enumerate(rows):
        if row is not None:
            tile = jnp.where(ids == r, jnp.broadcast_to(row, (TILE, LAT)), tile)
    return tile


def tile_freqs(t):
    return (TILE * t) // ND, (TILE * t + TILE - 1) // ND


def decayed_tiles(spectrum_ref, arrive):
    ids = row_ids()
    upper = ids < TILE // 2
    tiles = []
    sums = [jnp.zeros((TILE, LAT), F32) for _ in range(3)]
    for group in range(NF // 2):
        if group % 2 == 0:
            arrive(group // 2)
            for pair in range(GROUP_TILES):
                first = PART * (group // 2) + 16 * pair
                both = spectrum_ref[first : first + 16, :].astype(F32)
                tiles += [both[:TILE], both[TILE:]]
        nine = tiles[GROUP_TILES * group : GROUP_TILES * (group + 1)]
        low = (nine[0] + nine[1]) + (nine[2] + nine[3]) + jnp.where(upper, nine[4], 0.0)
        high = (nine[5] + nine[6]) + (nine[7] + nine[8]) + jnp.where(upper, 0.0, nine[4])
        for i, part in ((2 * group, low), (2 * group + 1, high)):
            weights = (AREA[i], AREA[i] / SIGMA[i], AREA[i] / math.sqrt(WAVENUM[i]))
            sums = [s + float(np.float32(w)) * part for s, w in zip(sums, weights)]
    moments = [jnp.broadcast_to(jnp.sum(s, axis=0, keepdims=True), (TILE, LAT)) for s in sums]
    mean_freq = moments[0] / moments[1]
    mean_wavenum = (moments[0] / moments[2]) ** 2
    steepness = moments[0] * mean_wavenum * mean_wavenum
    strength = mean_freq * (steepness / steep_ref) ** 2
    inverse = 1.0 / mean_wavenum
    factors = []
    for i in range(NF):
        ratio = float(np.float32(WAVENUM[i])) * inverse
        factors.append(jnp.exp(-dissip_rate * (strength * (0.5 * ratio + 0.5 * ratio * ratio))))
    out = []
    for t in range(BINS // TILE):
        if t % 2 == 0:
            both = spectrum_ref[TILE * t : TILE * t + 16, :].astype(F32)
        tile = both[:TILE] if t % 2 == 0 else both[TILE:]
        first, last = tile_freqs(t)
        factor = factors[first]
        if last != first:
            factor = jnp.where(upper, factor, factors[last])
        out.append(tile * factor)
    return out


def shared_tile(wind_ref, wet_ref, order):
    east, north, wet = split(wind_ref[0:1, :]), split(wind_ref[1:2, :]), split(wet_ref[0:1, :])
    column = jnp.full((1, LAT), order, jnp.int32).astype(F32)
    return stack_rows([None, *east, *north, *wet, column])


def fetch(section, spectrum_hbm, wind_hbm, wet_hbm, tables_hbm, spectrum_ref, wind_ref, wet_ref, table_ref, sems):
    me = lax.axis_index("sec") * section + lax.axis_index("dom")
    parts = [
        pltpu.make_async_copy(
            spectrum_hbm.at[pl.ds(PART * k, PART), :], spectrum_ref.at[pl.ds(PART * k, PART), :], sems.at[k]
        )
        for k in range(PARTS)
    ]
    rest = [
        pltpu.make_async_copy(source, target, sems.at[PARTS + k])
        for k, (source, target) in enumerate(
            ((wind_hbm, wind_ref), (wet_hbm, wet_ref), (tables_hbm.at[me], table_ref))
        )
    ]
    for copy in parts + rest:
        copy.start()

    def arrive(part):
        parts[part].wait()

    def arrive_rest():
        for copy in rest:
            copy.wait()

    return arrive, arrive_rest


def pack_kernel(
    devices, section, order_ref, spectrum_hbm, wind_hbm, wet_hbm, tables_hbm, out_ref, table_ref,
    spectrum_ref, wind_ref, wet_ref, sems,
):
    each, kept, rows = layout(devices)
    arrive, arrive_rest = fetch(
        section, spectrum_hbm, wind_hbm, wet_hbm, tables_hbm, spectrum_ref, wind_ref, wet_ref, table_ref, sems
    )
    tiles = decayed_tiles(spectrum_ref, arrive)
    arrive_rest()
    shared = shared_tile(wind_ref, wet_ref, order_ref[0])
    first = row_ids() == 0
    left = BINS - devices * each
    per = each // TILE
    for d in range(devices):
        last = shared
        if d < left:
            spare = tiles[per * devices + d // TILE]
            row = spare[d % TILE : d % TILE + 1]
            last = jnp.where(first, jnp.broadcast_to(row, (TILE, LAT)), shared)
        chunk = jnp.concatenate(tiles[per * d : per * (d + 1)] + [last], axis=0)
        out_ref[d] = chunk.astype(BF)


def loose_kernel(
    section, order_ref, spectrum_hbm, wind_hbm, wet_hbm, tables_hbm, out_ref, table_ref, shared_ref,
    spectrum_ref, wind_ref, wet_ref, sems,
):
    arrive, arrive_rest = fetch(
        section, spectrum_hbm, wind_hbm, wet_hbm, tables_hbm, spectrum_ref, wind_ref, wet_ref, table_ref, sems
    )
    tiles = decayed_tiles(spectrum_ref, arrive)
    arrive_rest()
    for pair in range(BINS // 16):
        both = jnp.concatenate(tiles[2 * pair : 2 * pair + 2], axis=0)
        out_ref[16 * pair : 16 * pair + 16, :] = both.astype(BF)
    shared_ref[...] = shared_tile(wind_ref, wet_ref, order_ref[0])


def packed(devices, section, block_order, spectrum, surface_wind, wet):
    each, kept, rows = layout(devices)
    shape = jax.ShapeDtypeStruct((devices, rows, LAT), BF)
    table_shape = jax.ShapeDtypeStruct((rows, LAT), F32)
    shared = dict(
        in_specs=[smem(), anywhere(), anywhere(), anywhere(), anywhere()],
        scratch_shapes=[
            pltpu.VMEM((BINS, LAT), BF),
            pltpu.VMEM((2, LAT), F32),
            pltpu.VMEM((1, LAT), F32),
            pltpu.SemaphoreType.DMA((PARTS + 3,)),
        ],
        compiler_params=pltpu.CompilerParams(vmem_limit_bytes=24 << 20),
    )
    operands = (block_order, spectrum, surface_wind, wet, jnp.asarray(device_tables(devices)))
    if each == kept:
        return pl.pallas_call(
            functools.partial(pack_kernel, devices, section),
            out_shape=(shape, table_shape),
            out_specs=(vmem(), vmem()),
            **shared,
        )(*operands)
    decayed, table, tile = pl.pallas_call(
        functools.partial(loose_kernel, section),
        out_shape=(
            jax.ShapeDtypeStruct((BINS, LAT), BF),
            table_shape,
            jax.ShapeDtypeStruct((TILE, LAT), F32),
        ),
        out_specs=(vmem(), vmem(), vmem()),
        **shared,
    )(*operands)
    main = decayed[: devices * each].reshape(devices, each, LAT)
    main = jnp.pad(main, ((0, 0), (0, kept - each), (0, 0)))
    spare = decayed[devices * each :]
    spare = jnp.pad(spare, ((0, devices - spare.shape[0]), (0, 0)))[:, None]
    common = jnp.broadcast_to(tile[1:].astype(BF)[None], (devices, TILE - 1, LAT))
    return jnp.concatenate([main, spare, common], axis=1), table


def lane_whole(rows):
    return lax.broadcasted_iota(jnp.int32, (rows, LAT), 1)


def own_stress(spectrum_ref, cosines, sines, east, north):
    upper = row_ids() < TILE // 2
    along = [c * east + s * north for c, s in zip(cosines, sines)]
    totals = [jnp.zeros((TILE, LAT), F32) for _ in range(GROUP_TILES)]

    def constant(values, first, last):
        low, high = float(np.float32(values[first])), float(np.float32(values[last]))
        return low if first == last else jnp.where(upper, low, high)

    for pair in range(BINS // 16):
        both = spectrum_ref[16 * pair : 16 * pair + 16, :].astype(F32)
        for half in range(2):
            t = 2 * pair + half
            p = t % GROUP_TILES
            tile = both[TILE * half : TILE * (half + 1)]
            slope = constant(1.2 / SPEED, *tile_freqs(t))
            weight = constant(stress_coef * AREA * SIGMA / SPEED, *tile_freqs(t))
            grown = jnp.maximum(0.0, slope * along[p] - 1.0)
            totals[p] = totals[p] + (weight * tile) * grown
    return [
        jnp.sum(sum(a * b for a, b in zip(parts, totals)), axis=0, keepdims=True)
        for parts in (cosines, sines)
    ]


def spread_kernel(
    devices, section, order_ref, recv_ref, spectrum_ref, table_ref, angle_ref, out_ref,
    field_a, field_b, wet_ref, numbers_ref, order_vmem, order_smem, slot_smem, sem,
):
    each, kept, rows = layout(devices)
    ids = row_ids()
    lane = lax.broadcasted_iota(jnp.int32, (TILE, LAT), 1)
    unit = math.gcd(devices, UNROLL)

    def every(body):
        if devices == unit:
            for column in range(devices):
                body(column)
            return

        def some(block, carry):
            for k in range(unit):
                body(block * unit + k)
            return carry

        lax.fori_loop(0, devices // unit, some, 0)

    span = min(LAT, devices)
    for block in range(devices // span):

        def place(s, tile, block=block):
            here = recv_ref[block * span + s, kept : kept + TILE, :].astype(F32)
            return jnp.where(lane == s, here, tile)

        orders = lax.fori_loop(0, span, place, jnp.zeros((TILE, LAT), F32), unroll=min(span, UNROLL))
        order_vmem[block] = orders.astype(jnp.int32)
    copy = pltpu.make_async_copy(order_vmem, order_smem, sem)
    copy.start()

    def weather(column):
        tile = recv_ref[column, kept : kept + TILE, :].astype(F32)
        return tile[1:2] + tile[2:3], tile[3:4] + tile[4:5], tile[5:6] + tile[6:7]

    def spread_lane(ref, t, k):
        return jnp.broadcast_to(ref[TILE * t : TILE * (t + 1), k : k + 1], (TILE, LAT))

    for t in range(rows // TILE):
        for k in range(8):
            numbers_ref[k, TILE * t : TILE * (t + 1), :] = spread_lane(table_ref, t, k)
    numbers_ref[6] = jnp.where(lane_whole(rows) == 0, 0.0, numbers_ref[6])
    numbers_ref[7] = jnp.where(lane_whole(rows) == LAT - 1, 0.0, numbers_ref[7])
    base = lax.axis_index("sec") * section
    angles = [[spread_lane(angle_ref, p, k) for p in range(GROUP_TILES)] for k in range(2)]
    stress = own_stress(spectrum_ref, *angles, *weather(base + order_ref[0])[:2])
    column_row = jnp.full((1, LAT), order_ref[0], jnp.int32).astype(F32)
    ending = stack_rows([None, *split(stress[0]), *split(stress[1]), None, None, column_row])
    copy.wait()

    def number(s):
        column = s // section * section + order_smem[s // span, TILE - 1, s % span]
        slot_smem[column] = s

    every(number)

    def renew(column):
        east, north, wet = weather(column)
        wet_ref[column] = jnp.broadcast_to(wet, (TILE, LAT))
        energy = recv_ref[slot_smem[column]].astype(F32)
        push = jnp.exp(jnp.maximum(0.0, numbers_ref[0] * east + numbers_ref[1] * north - numbers_ref[2]))
        field_a[column] = wet * energy * push

    every(renew)

    for substep in range(SUBSTEPS):
        source, target = (field_a, field_b) if substep % 2 == 0 else (field_b, field_a)
        for t in range(rows // TILE):
            part = pl.ds(TILE * t, TILE)
            keep, from_west, from_east, from_south, from_north = (
                numbers_ref[k, part, :] for k in range(3, 8)
            )

            def step(column):
                if isinstance(column, int):
                    west, east = (column - 1) % devices, (column + 1) % devices
                else:
                    west = jnp.where(column == 0, devices - 1, column - 1)
                    east = jnp.where(column == devices - 1, 0, column + 1)
                here = source[column, part, :]
                total = keep * here + from_west * source[west, part, :]
                total = total + from_east * source[east, part, :]
                total = total + from_south * pltpu.roll(here, 1, 1)
                total = total + from_north * pltpu.roll(here, LAT - 1, 1)
                target[column, part, :] = wet_ref[column] * total

            every(step)

    final = field_a if SUBSTEPS % 2 == 0 else field_b

    def finish(column):
        last = jnp.where(ids == 0, final[column, kept:, :], ending)
        whole = jnp.concatenate([final[column, :kept, :], last], axis=0)
        out_ref[slot_smem[column]] = whole.astype(BF)

    every(finish)


def spread(devices, section, block_order, received, spectrum, table):
    each, kept, rows = layout(devices)
    span = min(LAT, devices)
    return pl.pallas_call(
        functools.partial(spread_kernel, devices, section),
        out_shape=jax.ShapeDtypeStruct((devices, rows, LAT), BF),
        in_specs=[smem(), vmem(), vmem(), vmem(), vmem()],
        out_specs=vmem(),
        scratch_shapes=[
            pltpu.VMEM((devices, rows, LAT), F32),
            pltpu.VMEM((devices, rows, LAT), F32),
            pltpu.VMEM((devices, TILE, LAT), F32),
            pltpu.VMEM((8, rows, LAT), F32),
            pltpu.VMEM((devices // span, TILE, LAT), jnp.int32),
            pltpu.SMEM((devices // span, TILE, LAT), jnp.int32),
            pltpu.SMEM((devices,), jnp.int32),
            pltpu.SemaphoreType.DMA,
        ],
        compiler_params=pltpu.CompilerParams(vmem_limit_bytes=32 << 20),
    )(block_order, received, spectrum, table, jnp.asarray(angle_table()))


def collect(devices, section, returned_ref, wet_ref, stress_ref):
    each, kept, rows = layout(devices)
    base = lax.axis_index("sec") * section
    rank = lax.axis_index("dom").astype(F32)

    def pick(s, total):
        tile = returned_ref[base + s, kept : kept + TILE, :].astype(F32)
        mine = jnp.broadcast_to(tile[TILE - 1 : TILE] == rank, (TILE, LAT))
        return jnp.where(mine, tile, total)

    tile = lax.fori_loop(0, section, pick, jnp.zeros((TILE, LAT), F32), unroll=8)
    wet = wet_ref[0:1, :]
    stress_ref[0:1, :] = wet * (tile[1:2] + tile[2:3])
    stress_ref[1:2, :] = wet * (tile[3:4] + tile[4:5])


def unpack_kernel(devices, section, returned_ref, wet_ref, out_hbm, stress_ref, out_ref, sems):
    each, kept, rows = layout(devices)
    left = BINS - devices * each
    copies = []

    def leave(first, count):
        here = pl.ds(first, count)
        copies.append(pltpu.make_async_copy(out_ref.at[here, :], out_hbm.at[here, :], sems.at[len(copies)]))
        copies[-1].start()

    spare = []
    for tile in range(left // TILE):
        heads = [returned_ref[TILE * tile + r].astype(F32)[kept : kept + 1] for r in range(TILE)]
        spare.append(stack_rows(heads))
    out_ref[devices * each :, :] = jnp.concatenate(spare, axis=0).astype(BF)
    leave(devices * each, left)
    share = devices // 2 // LEAVING
    for pair in range(devices // 2):
        both = [returned_ref[2 * pair + half].astype(F32)[:each] for half in range(2)]
        out_ref[2 * each * pair : 2 * each * (pair + 1), :] = jnp.concatenate(both, axis=0).astype(BF)
        if pair % share == share - 1:
            leave(2 * each * (pair - share + 1), 2 * each * share)
    collect(devices, section, returned_ref, wet_ref, stress_ref)
    for copy in copies:
        copy.wait()


def unpacked(devices, section, returned, wet):
    each, kept, rows = layout(devices)
    left = BINS - devices * each
    stress_shape = jax.ShapeDtypeStruct((2, LAT), F32)
    params = pltpu.CompilerParams(vmem_limit_bytes=24 << 20)
    if each == kept and devices % (2 * LEAVING) == 0 and left > 0 and left % 16 == 0:
        return pl.pallas_call(
            functools.partial(unpack_kernel, devices, section),
            out_shape=(jax.ShapeDtypeStruct((BINS, LAT), BF), stress_shape),
            in_specs=[vmem(), vmem()],
            out_specs=(anywhere(), vmem()),
            scratch_shapes=[
                pltpu.VMEM((BINS, LAT), BF),
                pltpu.SemaphoreType.DMA((LEAVING + 1,)),
            ],
            compiler_params=params,
        )(returned, wet)
    stress = pl.pallas_call(
        functools.partial(collect, devices, section),
        out_shape=stress_shape,
        in_specs=[vmem(), vmem()],
        out_specs=vmem(),
        compiler_params=params,
    )(returned, wet)
    main = returned[:, :each].reshape(devices * each, LAT)
    return jnp.concatenate([main, returned[:left, kept]], axis=0), stress


def on_device(devices, section, spectrum, surface_wind, wet_mask, block_order):
    wet = wet_mask.reshape(1, LAT)
    sending, table = packed(devices, section, block_order, spectrum, surface_wind, wet)
    received = lax.all_to_all(sending, AXES, split_axis=0, concat_axis=0, tiled=True)
    leaving = spread(devices, section, block_order, received, spectrum, table)
    returned = lax.all_to_all(leaving, AXES, split_axis=0, concat_axis=0, tiled=True)
    return unpacked(devices, section, returned, wet)


def solution(mesh):
    section = mesh.shape["dom"]
    devices = mesh.shape["sec"] * section
    placed = (P(None, AXES), P(None, AXES), P(AXES), P(AXES))
    return jax.shard_map(
        functools.partial(on_device, devices, section),
        mesh=mesh,
        in_specs=placed,
        out_specs=(P(None, AXES), P(None, AXES)),
        check_vma=False,
    )
```

```python
import functools
import math

import jax
import jax.numpy as jnp
import numpy as np
from jax import lax
from jax.experimental import pallas as pl
from jax.experimental.pallas import tpu as pltpu
from jax.sharding import PartitionSpec as P

NF = 36
ND = 36
BINS = NF * ND
LAT = 128
SUBSTEPS = 4

gravity = 9.81
base_freq = 0.035
freq_growth = 1.1
wind_rate = 0.015
dissip_rate = 0.008
steep_ref = 3.0
stress_coef = 0.01
courant = 0.62

AXES = ("sec", "dom")
TILE = 8
UNROLL = 32
BATCH = 8
PART = 144
PARTS = BINS // PART
GROUP_TILES = 9
BF = jnp.bfloat16
F32 = jnp.float32

FREQ = np.arange(NF, dtype=np.float64)
SIGMA = 2.0 * math.pi * base_freq * freq_growth**FREQ
WAVENUM = SIGMA * SIGMA / gravity
SPEED = gravity / SIGMA
AREA = 0.1 * SIGMA * (2.0 * math.pi / ND)
THETA = 2.0 * math.pi * np.arange(ND, dtype=np.float64) / ND
COS, SIN = (np.where(np.abs(wave) < 1e-9, 0.0, wave) for wave in (np.cos(THETA), np.sin(THETA)))


def vmem():
    return pl.BlockSpec(memory_space=pltpu.VMEM)


def smem():
    return pl.BlockSpec(memory_space=pltpu.SMEM)


def hbm():
    return pl.BlockSpec(memory_space=pltpu.HBM)


def layout(devices):
    each = BINS // devices
    rows = -(-(each + TILE) // 16) * 16
    return each, rows - TILE, rows


def tile_slots(devices):
    each, kept, rows = layout(devices)
    if each != kept:
        return None, 0
    count, half = each // TILE, devices // 2
    ways = [[], [], []]
    for t in range(devices * count):
        wave = SIN[(TILE * t + np.arange(TILE)) % ND]
        ways[0 if (wave >= 0).all() else 1 if (wave <= 0).all() else 2].append(t)
    sure = min(len(ways[0]) // half, len(ways[1]) // half, count)
    rest = sorted(ways[0][sure * half :] + ways[1][sure * half :] + ways[2])
    slots = []
    for d in range(devices):
        way, place = ways[d // half], d % half
        mixed = rest[(count - sure) * d : (count - sure) * (d + 1)]
        slots.append(way[sure * place : sure * (place + 1)] + mixed)
    return slots, sure


def spare_way(devices):
    wave = SIN[np.arange(BINS // devices * devices, BINS) % ND]
    return 1 if (wave >= 0).all() else -1 if (wave <= 0).all() else 0


def device_tables(devices):
    each, kept, rows = layout(devices)
    slots = tile_slots(devices)[0]
    table = np.zeros((devices, rows, LAT), np.float64)
    for device in range(devices):
        bins = np.full((rows,), -1)
        if slots is None:
            bins[:each] = device * each + np.arange(each)
        else:
            bins[:each] = (TILE * np.array(slots[device])[:, None] + np.arange(TILE)).reshape(-1)
        if devices * each + device < BINS:
            bins[kept] = devices * each + device
        real = bins >= 0
        i, j = np.maximum(bins, 0) // ND, np.maximum(bins, 0) % ND
        scale = wind_rate * SIGMA[i]
        travel = courant * freq_growth ** (-i.astype(np.float64))
        cx, cy = travel * COS[j], travel * SIN[j]
        values = (
            scale * 1.2 / SPEED[i] * COS[j],
            scale * 1.2 / SPEED[i] * SIN[j],
            scale,
            1.0 - np.abs(cx) - np.abs(cy),
            np.maximum(cx, 0.0),
            np.maximum(-cx, 0.0),
            np.maximum(cy, 0.0),
            np.maximum(-cy, 0.0),
        )
        for lane, value in enumerate(values):
            table[device, :, lane] = np.where(real, value, 0.0)
    return table.astype(np.float32)


def angle_table():
    table = np.zeros((GROUP_TILES * TILE, LAT), np.float64)
    angle = np.arange(GROUP_TILES * TILE) % ND
    table[:, 0], table[:, 1] = COS[angle], SIN[angle]
    return table.astype(np.float32)


def split(value):
    high = value.astype(BF)
    return high.astype(F32), (value - high.astype(F32)).astype(BF).astype(F32)


def row_ids():
    return lax.broadcasted_iota(jnp.int32, (TILE, LAT), 0)


def stack_rows(rows):
    ids = row_ids()
    tile = jnp.zeros((TILE, LAT), F32)
    for r, row in enumerate(rows):
        if row is not None:
            tile = jnp.where(ids == r, jnp.broadcast_to(row, (TILE, LAT)), tile)
    return tile


def tile_freqs(t):
    return (TILE * t) // ND, (TILE * t + TILE - 1) // ND


def decayed_tiles(spectrum_ref, arrive):
    ids = row_ids()
    upper = ids < TILE // 2
    tiles = []
    sums = [jnp.zeros((TILE, LAT), F32) for _ in range(3)]
    for group in range(NF // 2):
        if group % 2 == 0:
            arrive(group // 2)
            for pair in range(GROUP_TILES):
                first = PART * (group // 2) + 16 * pair
                both = spectrum_ref[first : first + 16, :].astype(F32)
                tiles += [both[:TILE], both[TILE:]]
        nine = tiles[GROUP_TILES * group : GROUP_TILES * (group + 1)]
        low = (nine[0] + nine[1]) + (nine[2] + nine[3]) + jnp.where(upper, nine[4], 0.0)
        high = (nine[5] + nine[6]) + (nine[7] + nine[8]) + jnp.where(upper, 0.0, nine[4])
        for i, part in ((2 * group, low), (2 * group + 1, high)):
            weights = (AREA[i], AREA[i] / SIGMA[i], AREA[i] / math.sqrt(WAVENUM[i]))
            sums = [s + float(np.float32(w)) * part for s, w in zip(sums, weights)]
    moments = [jnp.broadcast_to(jnp.sum(s, axis=0, keepdims=True), (TILE, LAT)) for s in sums]
    mean_freq = moments[0] / moments[1]
    mean_wavenum = (moments[0] / moments[2]) ** 2
    steepness = moments[0] * mean_wavenum * mean_wavenum
    strength = mean_freq * (steepness / steep_ref) ** 2
    inverse = 1.0 / mean_wavenum
    factors = []
    for i in range(NF):
        ratio = float(np.float32(WAVENUM[i])) * inverse
        factors.append(jnp.exp(-dissip_rate * (strength * (0.5 * ratio + 0.5 * ratio * ratio))))

    def decayed(t):
        first, last = tile_freqs(t)
        factor = factors[first]
        if last != first:
            factor = jnp.where(upper, factor, factors[last])
        return spectrum_ref[TILE * t : TILE * (t + 1), :].astype(F32) * factor

    return decayed


def shared_tile(wind_ref, wet_ref, order):
    east, north, wet = split(wind_ref[0:1, :]), split(wind_ref[1:2, :]), split(wet_ref[0:1, :])
    column = jnp.full((1, LAT), order, jnp.int32).astype(F32)
    return stack_rows([None, *east, *north, *wet, column])


def fetch(section, spectrum_hbm, wind_hbm, wet_hbm, tables_hbm, spectrum_ref, wind_ref, wet_ref, table_ref, sems):
    me = lax.axis_index("sec") * section + lax.axis_index("dom")
    parts = [
        pltpu.make_async_copy(
            spectrum_hbm.at[pl.ds(PART * k, PART), :], spectrum_ref.at[pl.ds(PART * k, PART), :], sems.at[k]
        )
        for k in range(PARTS)
    ]
    rest = [
        pltpu.make_async_copy(source, target, sems.at[PARTS + k])
        for k, (source, target) in enumerate(
            ((wind_hbm, wind_ref), (wet_hbm, wet_ref), (tables_hbm.at[me], table_ref))
        )
    ]
    for copy in parts + rest:
        copy.start()

    def arrive(part):
        parts[part].wait()

    def arrive_rest():
        for copy in rest:
            copy.wait()

    return arrive, arrive_rest


def pack_kernel(
    devices, section, order_ref, spectrum_hbm, wind_hbm, wet_hbm, tables_hbm, out_ref, table_ref,
    spectrum_ref, wind_ref, wet_ref, sems,
):
    each, kept, rows = layout(devices)
    arrive, arrive_rest = fetch(
        section, spectrum_hbm, wind_hbm, wet_hbm, tables_hbm, spectrum_ref, wind_ref, wet_ref, table_ref, sems
    )
    decayed = decayed_tiles(spectrum_ref, arrive)
    arrive_rest()
    shared = shared_tile(wind_ref, wet_ref, order_ref[0])
    first = row_ids() == 0
    left = BINS - devices * each
    slots = tile_slots(devices)[0]
    spares = [decayed(t) for t in range(devices * each // TILE, BINS // TILE)]
    for d in range(devices):
        last = shared
        if d < left:
            row = spares[d // TILE][d % TILE : d % TILE + 1]
            last = jnp.where(first, jnp.broadcast_to(row, (TILE, LAT)), shared)
        chunk = jnp.concatenate([decayed(t) for t in slots[d]] + [last], axis=0)
        out_ref[d] = chunk.astype(BF)


def loose_kernel(
    section, order_ref, spectrum_hbm, wind_hbm, wet_hbm, tables_hbm, out_ref, table_ref, shared_ref,
    spectrum_ref, wind_ref, wet_ref, sems,
):
    arrive, arrive_rest = fetch(
        section, spectrum_hbm, wind_hbm, wet_hbm, tables_hbm, spectrum_ref, wind_ref, wet_ref, table_ref, sems
    )
    decayed = decayed_tiles(spectrum_ref, arrive)
    arrive_rest()
    for pair in range(BINS // 16):
        both = jnp.concatenate([decayed(2 * pair), decayed(2 * pair + 1)], axis=0)
        out_ref[16 * pair : 16 * pair + 16, :] = both.astype(BF)
    shared_ref[...] = shared_tile(wind_ref, wet_ref, order_ref[0])


def packed(devices, section, block_order, spectrum, surface_wind, wet):
    each, kept, rows = layout(devices)
    shape = jax.ShapeDtypeStruct((devices, rows, LAT), BF)
    table_shape = jax.ShapeDtypeStruct((rows, LAT), F32)
    shared = dict(
        in_specs=[smem(), hbm(), hbm(), hbm(), hbm()],
        scratch_shapes=[
            pltpu.VMEM((BINS, LAT), BF),
            pltpu.VMEM((2, LAT), F32),
            pltpu.VMEM((1, LAT), F32),
            pltpu.SemaphoreType.DMA((PARTS + 3,)),
        ],
        compiler_params=pltpu.CompilerParams(vmem_limit_bytes=60 << 20),
    )
    operands = (block_order, spectrum, surface_wind, wet, jnp.asarray(device_tables(devices)))
    if each == kept:
        return pl.pallas_call(
            functools.partial(pack_kernel, devices, section),
            out_shape=(shape, table_shape),
            out_specs=(vmem(), vmem()),
            **shared,
        )(*operands)
    decayed, table, tile = pl.pallas_call(
        functools.partial(loose_kernel, section),
        out_shape=(
            jax.ShapeDtypeStruct((BINS, LAT), BF),
            table_shape,
            jax.ShapeDtypeStruct((TILE, LAT), F32),
        ),
        out_specs=(vmem(), vmem(), vmem()),
        **shared,
    )(*operands)
    main = decayed[: devices * each].reshape(devices, each, LAT)
    main = jnp.pad(main, ((0, 0), (0, kept - each), (0, 0)))
    spare = decayed[devices * each :]
    spare = jnp.pad(spare, ((0, devices - spare.shape[0]), (0, 0)))[:, None]
    common = jnp.broadcast_to(tile[1:].astype(BF)[None], (devices, TILE - 1, LAT))
    return jnp.concatenate([main, spare, common], axis=1), table


def lane_whole(rows):
    return lax.broadcasted_iota(jnp.int32, (rows, LAT), 1)


def own_stress(spectrum_ref, cosines, sines, east, north):
    upper = row_ids() < TILE // 2
    along = [c * east + s * north for c, s in zip(cosines, sines)]
    totals = [jnp.zeros((TILE, LAT), F32) for _ in range(GROUP_TILES)]

    def constant(values, first, last):
        low, high = float(np.float32(values[first])), float(np.float32(values[last]))
        return low if first == last else jnp.where(upper, low, high)

    for pair in range(BINS // 16):
        both = spectrum_ref[16 * pair : 16 * pair + 16, :].astype(F32)
        for half in range(2):
            t = 2 * pair + half
            p = t % GROUP_TILES
            tile = both[TILE * half : TILE * (half + 1)]
            slope = constant(1.2 / SPEED, *tile_freqs(t))
            weight = constant(stress_coef * AREA * SIGMA / SPEED, *tile_freqs(t))
            grown = jnp.maximum(0.0, slope * along[p] - 1.0)
            totals[p] = totals[p] + (weight * tile) * grown
    return [
        jnp.sum(sum(a * b for a, b in zip(parts, totals)), axis=0, keepdims=True)
        for parts in (cosines, sines)
    ]


def spread_kernel(
    devices, section, order_ref, recv_ref, spectrum_ref, table_ref, angle_ref, out_ref,
    field_a, field_b, wet_ref, numbers_ref, slot_smem,
):
    each, kept, rows = layout(devices)
    ids = row_ids()
    lane = lax.broadcasted_iota(jnp.int32, (TILE, LAT), 1)
    unit = math.gcd(devices, UNROLL)

    def every(body, batch=1):
        if devices == unit:
            for k in range(0, unit, batch):
                body(*range(k, k + batch))
            return

        def some(block, carry):
            for k in range(0, unit, batch):
                body(*(block * unit + k + n for n in range(batch)))
            return carry

        lax.fori_loop(0, devices // unit, some, 0)

    span = min(LAT, devices)
    for block in range(devices // span):

        def place(s, tile, block=block):
            here = recv_ref[block * span + s, kept : kept + TILE, :].astype(F32)
            return jnp.where(lane == s, here, tile)

        orders = lax.fori_loop(0, span, place, jnp.zeros((TILE, LAT), F32), unroll=min(span, UNROLL))
        last = orders[TILE - 1 :].astype(jnp.int32)
        for s in range(span):
            slot_smem[(block * span + s) // section * section + last[0, s]] = block * span + s

    def weather(column):
        tile = recv_ref[column, kept : kept + TILE, :].astype(F32)
        return tile[1:2] + tile[2:3], tile[3:4] + tile[4:5], tile[5:6] + tile[6:7]

    def spread_lane(ref, t, k):
        return jnp.broadcast_to(ref[TILE * t : TILE * (t + 1), k : k + 1], (TILE, LAT))

    for t in range(rows // TILE):
        for k in range(8):
            numbers_ref[k, TILE * t : TILE * (t + 1), :] = spread_lane(table_ref, t, k)
    numbers_ref[6] = jnp.where(lane_whole(rows) == 0, 0.0, numbers_ref[6])
    numbers_ref[7] = jnp.where(lane_whole(rows) == LAT - 1, 0.0, numbers_ref[7])
    base = lax.axis_index("sec") * section
    me = base + lax.axis_index("dom")
    angles = [[spread_lane(angle_ref, p, k) for p in range(GROUP_TILES)] for k in range(2)]
    stress = own_stress(spectrum_ref, *angles, *weather(base + order_ref[0])[:2])
    column_row = jnp.full((1, LAT), order_ref[0], jnp.int32).astype(F32)
    ending = stack_rows([None, *split(stress[0]), *split(stress[1]), None, None, column_row])
    def renew(column):
        east, north, wet = weather(column)
        wet_ref[column] = jnp.broadcast_to(wet, (TILE, LAT))
        energy = recv_ref[slot_smem[column]].astype(F32)
        push = jnp.exp(jnp.maximum(0.0, numbers_ref[0] * east + numbers_ref[1] * north - numbers_ref[2]))
        field_a[column] = wet * energy * push

    every(renew)

    def around(column):
        if isinstance(column, int):
            return (column - 1) % devices, (column + 1) % devices
        return jnp.where(column == 0, devices - 1, column - 1), jnp.where(column == devices - 1, 0, column + 1)

    sure = tile_slots(devices)[1]
    northward = me < devices // 2

    def mover(source, t):
        part = pl.ds(TILE * t, TILE)
        keep, from_west, from_east, from_south, from_north = (numbers_ref[k, part, :] for k in range(3, 8))
        westerly, southerly = from_west > 0.0, from_south > 0.0
        from_x, from_y = from_west + from_east, from_south + from_north
        way = spare_way(devices) if TILE * t == kept else 0

        def shifted(here):
            if t < sure:
                return pltpu.roll(here, jnp.where(northward, 1, LAT - 1), 1)
            if way:
                return pltpu.roll(here, way % LAT, 1)
            return jnp.where(southerly, pltpu.roll(here, 1, 1), pltpu.roll(here, LAT - 1, 1))

        def moved(column):
            west, east = around(column)
            here = source[column, part, :]
            total = keep * here + from_x * jnp.where(westerly, source[west, part, :], source[east, part, :])
            return wet_ref[column] * (total + from_y * shifted(here))

        return moved

    for substep in range(SUBSTEPS - 1):
        source, target = (field_a, field_b) if substep % 2 == 0 else (field_b, field_a)
        for t in range(rows // TILE):
            moved = mover(source, t)

            def step(column):
                target[column, TILE * t : TILE * (t + 1), :] = moved(column)

            every(step)

    source = field_a if (SUBSTEPS - 1) % 2 == 0 else field_b
    for t in range(0, rows // TILE, 2):
        upper_tile, lower_tile = mover(source, t), mover(source, t + 1)

        def finish(*columns):
            made = []
            for column in columns:
                upper, lower = upper_tile(column), lower_tile(column)
                if TILE * (t + 1) == kept:
                    lower = jnp.where(ids == 0, lower, ending)
                made.append(jnp.concatenate([upper, lower], axis=0).astype(BF))
            for column, value in zip(columns, made):
                out_ref[slot_smem[column], TILE * t : TILE * (t + 2), :] = value

        every(finish, min(BATCH, unit))


def spread(devices, section, block_order, received, spectrum, table):
    each, kept, rows = layout(devices)
    span = min(LAT, devices)
    return pl.pallas_call(
        functools.partial(spread_kernel, devices, section),
        out_shape=jax.ShapeDtypeStruct((devices, rows, LAT), BF),
        in_specs=[smem(), vmem(), vmem(), vmem(), vmem()],
        out_specs=vmem(),
        scratch_shapes=[
            pltpu.VMEM((devices, rows, LAT), F32),
            pltpu.VMEM((devices, rows, LAT), F32),
            pltpu.VMEM((devices, TILE, LAT), F32),
            pltpu.VMEM((8, rows, LAT), F32),
            pltpu.SMEM((devices,), jnp.int32),
        ],
        compiler_params=pltpu.CompilerParams(vmem_limit_bytes=32 << 20),
    )(block_order, received, spectrum, table, jnp.asarray(angle_table()))


def collect(devices, section, returned_ref, wet_ref, stress_ref):
    each, kept, rows = layout(devices)
    base = lax.axis_index("sec") * section
    rank = lax.axis_index("dom").astype(F32)

    def pick(s, total):
        tile = returned_ref[base + s, kept : kept + TILE, :].astype(F32)
        mine = jnp.broadcast_to(tile[TILE - 1 : TILE] == rank, (TILE, LAT))
        return jnp.where(mine, tile, total)

    tile = lax.fori_loop(0, section, pick, jnp.zeros((TILE, LAT), F32), unroll=8)
    wet = wet_ref[0:1, :]
    stress_ref[0:1, :] = wet * (tile[1:2] + tile[2:3])
    stress_ref[1:2, :] = wet * (tile[3:4] + tile[4:5])


def unpack_kernel(devices, section, returned_ref, wet_ref, out_ref, stress_ref):
    each, kept, rows = layout(devices)
    left = BINS - devices * each
    home = {t: (d, k) for d, tiles in enumerate(tile_slots(devices)[0]) for k, t in enumerate(tiles)}
    for pair in range(devices * each // 16):
        for t in (2 * pair, 2 * pair + 1):
            d, k = home[t]
            out_ref[TILE * t : TILE * (t + 1), :] = returned_ref[d, TILE * k : TILE * (k + 1), :]
    spare = []
    for tile in range(left // TILE):
        heads = [returned_ref[TILE * tile + r].astype(F32)[kept : kept + 1] for r in range(TILE)]
        spare.append(stack_rows(heads))
    out_ref[devices * each :, :] = jnp.concatenate(spare, axis=0).astype(BF)
    collect(devices, section, returned_ref, wet_ref, stress_ref)


def unpacked(devices, section, returned, wet):
    each, kept, rows = layout(devices)
    left = BINS - devices * each
    stress_shape = jax.ShapeDtypeStruct((2, LAT), F32)
    params = pltpu.CompilerParams(vmem_limit_bytes=24 << 20)
    if each == kept and devices % 2 == 0 and each % TILE == 0 and left % 16 == 0:
        return pl.pallas_call(
            functools.partial(unpack_kernel, devices, section),
            out_shape=(jax.ShapeDtypeStruct((BINS, LAT), BF), stress_shape),
            in_specs=[vmem(), vmem()],
            out_specs=(vmem(), vmem()),
            compiler_params=params,
        )(returned, wet)
    stress = pl.pallas_call(
        functools.partial(collect, devices, section),
        out_shape=stress_shape,
        in_specs=[vmem(), vmem()],
        out_specs=vmem(),
        compiler_params=params,
    )(returned, wet)
    main = returned[:, :each].reshape(devices * each, LAT)
    return jnp.concatenate([main, returned[:left, kept]], axis=0), stress


def on_device(devices, section, spectrum, surface_wind, wet_mask, block_order):
    wet = wet_mask.reshape(1, LAT)
    sending, table = packed(devices, section, block_order, spectrum, surface_wind, wet)
    received = lax.all_to_all(sending, AXES, split_axis=0, concat_axis=0, tiled=True)
    leaving = spread(devices, section, block_order, received, spectrum, table)
    returned = lax.all_to_all(leaving, AXES, split_axis=0, concat_axis=0, tiled=True)
    return unpacked(devices, section, returned, wet)


def solution(mesh):
    section = mesh.shape["dom"]
    devices = mesh.shape["sec"] * section
    placed = (P(None, AXES), P(None, AXES), P(AXES), P(AXES))
    return jax.shard_map(
        functools.partial(on_device, devices, section),
        mesh=mesh,
        in_specs=placed,
        out_specs=(P(None, AXES), P(None, AXES)),
        check_vma=False,
    )
```

```python
import functools
import math

import jax
import jax.numpy as jnp
import numpy as np
from jax import lax
from jax.experimental import pallas as pl
from jax.experimental.pallas import tpu as pltpu
from jax.sharding import PartitionSpec as P

NF = 36
ND = 36
BINS = NF * ND
LAT = 128
SUBSTEPS = 4

gravity = 9.81
base_freq = 0.035
freq_growth = 1.1
wind_rate = 0.015
dissip_rate = 0.008
steep_ref = 3.0
stress_coef = 0.01
courant = 0.62

AXES = ("sec", "dom")
TILE = 8
QUAD = 4
UNROLL = 32
BATCH = 8
PART = 144
PARTS = BINS // PART
GROUP_TILES = 9
BF = jnp.bfloat16
F32 = jnp.float32

FREQ = np.arange(NF, dtype=np.float64)
SIGMA = 2.0 * math.pi * base_freq * freq_growth**FREQ
WAVENUM = SIGMA * SIGMA / gravity
SPEED = gravity / SIGMA
AREA = 0.1 * SIGMA * (2.0 * math.pi / ND)
THETA = 2.0 * math.pi * np.arange(ND, dtype=np.float64) / ND
COS, SIN = (np.where(np.abs(wave) < 1e-9, 0.0, wave) for wave in (np.cos(THETA), np.sin(THETA)))


def vmem():
    return pl.BlockSpec(memory_space=pltpu.VMEM)


def smem():
    return pl.BlockSpec(memory_space=pltpu.SMEM)


def hbm():
    return pl.BlockSpec(memory_space=pltpu.HBM)


def layout(devices):
    each = BINS // devices
    rows = -(-(each + TILE) // 16) * 16
    return each, rows - TILE, rows


def tile_slots(devices):
    each, kept, rows = layout(devices)
    if each != kept:
        return None, 0
    count, half = each // TILE, devices // 2
    ways = [[], [], []]
    for t in range(devices * count):
        wave = SIN[(TILE * t + np.arange(TILE)) % ND]
        ways[0 if (wave >= 0).all() else 1 if (wave <= 0).all() else 2].append(t)
    sure = min(len(ways[0]) // half, len(ways[1]) // half, count)
    rest = sorted(ways[0][sure * half :] + ways[1][sure * half :] + ways[2])
    slots = []
    for d in range(devices):
        way, place = ways[d // half], d % half
        mixed = rest[(count - sure) * d : (count - sure) * (d + 1)]
        slots.append(way[sure * place : sure * (place + 1)] + mixed)
    return slots, sure


def spare_way(devices):
    wave = SIN[np.arange(BINS // devices * devices, BINS) % ND]
    return 1 if (wave >= 0).all() else -1 if (wave <= 0).all() else 0


def device_tables(devices):
    each, kept, rows = layout(devices)
    slots = tile_slots(devices)[0]
    table = np.zeros((devices, rows, LAT), np.float64)
    for device in range(devices):
        bins = np.full((rows,), -1)
        if slots is None:
            bins[:each] = device * each + np.arange(each)
        else:
            bins[:each] = (TILE * np.array(slots[device])[:, None] + np.arange(TILE)).reshape(-1)
        if devices * each + device < BINS:
            bins[kept] = devices * each + device
        real = bins >= 0
        i, j = np.maximum(bins, 0) // ND, np.maximum(bins, 0) % ND
        scale = wind_rate * SIGMA[i]
        travel = courant * freq_growth ** (-i.astype(np.float64))
        cx, cy = travel * COS[j], travel * SIN[j]
        values = (
            scale * 1.2 / SPEED[i] * COS[j],
            scale * 1.2 / SPEED[i] * SIN[j],
            scale,
            1.0 - np.abs(cx) - np.abs(cy),
            np.maximum(cx, 0.0),
            np.maximum(-cx, 0.0),
            np.maximum(cy, 0.0),
            np.maximum(-cy, 0.0),
        )
        for lane, value in enumerate(values):
            table[device, :, lane] = np.where(real, value, 0.0)
    return table.astype(np.float32)


def angle_table():
    table = np.zeros((GROUP_TILES * TILE, LAT), np.float64)
    angle = np.arange(GROUP_TILES * TILE) % ND
    table[:, 0], table[:, 1] = COS[angle], SIN[angle]
    return table.astype(np.float32)


def split(value):
    high = value.astype(BF)
    return high.astype(F32), (value - high.astype(F32)).astype(BF).astype(F32)


def row_ids():
    return lax.broadcasted_iota(jnp.int32, (TILE, LAT), 0)


def stack_rows(rows):
    ids = row_ids()
    tile = jnp.zeros((TILE, LAT), F32)
    for r, row in enumerate(rows):
        if row is not None:
            tile = jnp.where(ids == r, jnp.broadcast_to(row, (TILE, LAT)), tile)
    return tile


def tile_freqs(t):
    return (TILE * t) // ND, (TILE * t + TILE - 1) // ND


def decayed_tiles(spectrum_ref, arrive):
    ids = row_ids()
    upper = ids < TILE // 2
    tiles = []
    sums = [jnp.zeros((TILE, LAT), F32) for _ in range(3)]
    for group in range(NF // 2):
        if group % 2 == 0:
            arrive(group // 2)
            for pair in range(GROUP_TILES):
                first = PART * (group // 2) + 16 * pair
                both = spectrum_ref[first : first + 16, :].astype(F32)
                tiles += [both[:TILE], both[TILE:]]
        nine = tiles[GROUP_TILES * group : GROUP_TILES * (group + 1)]
        low = (nine[0] + nine[1]) + (nine[2] + nine[3]) + jnp.where(upper, nine[4], 0.0)
        high = (nine[5] + nine[6]) + (nine[7] + nine[8]) + jnp.where(upper, 0.0, nine[4])
        for i, part in ((2 * group, low), (2 * group + 1, high)):
            weights = (AREA[i], AREA[i] / SIGMA[i], AREA[i] / math.sqrt(WAVENUM[i]))
            sums = [s + float(np.float32(w)) * part for s, w in zip(sums, weights)]
    moments = [jnp.broadcast_to(jnp.sum(s, axis=0, keepdims=True), (TILE, LAT)) for s in sums]
    mean_freq = moments[0] / moments[1]
    mean_wavenum = (moments[0] / moments[2]) ** 2
    steepness = moments[0] * mean_wavenum * mean_wavenum
    strength = mean_freq * (steepness / steep_ref) ** 2
    inverse = 1.0 / mean_wavenum
    factors = []
    for i in range(NF):
        ratio = float(np.float32(WAVENUM[i])) * inverse
        factors.append(jnp.exp(-dissip_rate * (strength * (0.5 * ratio + 0.5 * ratio * ratio))))

    def decayed(t):
        first, last = tile_freqs(t)
        factor = factors[first]
        if last != first:
            factor = jnp.where(upper, factor, factors[last])
        return spectrum_ref[TILE * t : TILE * (t + 1), :].astype(F32) * factor

    return decayed


def shared_tile(wind_ref, wet_ref, order):
    east, north, wet = split(wind_ref[0:1, :]), split(wind_ref[1:2, :]), split(wet_ref[0:1, :])
    column = jnp.full((1, LAT), order, jnp.int32).astype(F32)
    return stack_rows([None, *east, *north, *wet, column])


def fetch(section, spectrum_hbm, wind_hbm, wet_hbm, tables_hbm, spectrum_ref, wind_ref, wet_ref, table_ref, sems):
    me = lax.axis_index("sec") * section + lax.axis_index("dom")
    parts = [
        pltpu.make_async_copy(
            spectrum_hbm.at[pl.ds(PART * k, PART), :], spectrum_ref.at[pl.ds(PART * k, PART), :], sems.at[k]
        )
        for k in range(PARTS)
    ]
    rest = [
        pltpu.make_async_copy(source, target, sems.at[PARTS + k])
        for k, (source, target) in enumerate(
            ((wind_hbm, wind_ref), (wet_hbm, wet_ref), (tables_hbm.at[me], table_ref))
        )
    ]
    for copy in parts + rest:
        copy.start()

    def arrive(part):
        parts[part].wait()

    def arrive_rest():
        for copy in rest:
            copy.wait()

    return arrive, arrive_rest


def pack_kernel(
    devices, section, order_ref, spectrum_hbm, wind_hbm, wet_hbm, tables_hbm, out_ref, table_ref,
    spectrum_ref, wind_ref, wet_ref, sems,
):
    each, kept, rows = layout(devices)
    arrive, arrive_rest = fetch(
        section, spectrum_hbm, wind_hbm, wet_hbm, tables_hbm, spectrum_ref, wind_ref, wet_ref, table_ref, sems
    )
    decayed = decayed_tiles(spectrum_ref, arrive)
    arrive_rest()
    shared = shared_tile(wind_ref, wet_ref, order_ref[0])
    first = row_ids() == 0
    left = BINS - devices * each
    slots = tile_slots(devices)[0]
    spares = [decayed(t) for t in range(devices * each // TILE, BINS // TILE)]
    for d in range(devices):
        last = shared
        if d < left:
            row = spares[d // TILE][d % TILE : d % TILE + 1]
            last = jnp.where(first, jnp.broadcast_to(row, (TILE, LAT)), shared)
        chunk = jnp.concatenate([decayed(t) for t in slots[d]] + [last], axis=0)
        out_ref[d] = chunk.astype(BF)


def loose_kernel(
    section, order_ref, spectrum_hbm, wind_hbm, wet_hbm, tables_hbm, out_ref, table_ref, shared_ref,
    spectrum_ref, wind_ref, wet_ref, sems,
):
    arrive, arrive_rest = fetch(
        section, spectrum_hbm, wind_hbm, wet_hbm, tables_hbm, spectrum_ref, wind_ref, wet_ref, table_ref, sems
    )
    decayed = decayed_tiles(spectrum_ref, arrive)
    arrive_rest()
    for pair in range(BINS // 16):
        both = jnp.concatenate([decayed(2 * pair), decayed(2 * pair + 1)], axis=0)
        out_ref[16 * pair : 16 * pair + 16, :] = both.astype(BF)
    shared_ref[...] = shared_tile(wind_ref, wet_ref, order_ref[0])


def packed(devices, section, block_order, spectrum, surface_wind, wet):
    each, kept, rows = layout(devices)
    shape = jax.ShapeDtypeStruct((devices, rows, LAT), BF)
    table_shape = jax.ShapeDtypeStruct((rows, LAT), F32)
    shared = dict(
        in_specs=[smem(), hbm(), hbm(), hbm(), hbm()],
        scratch_shapes=[
            pltpu.VMEM((BINS, LAT), BF),
            pltpu.VMEM((2, LAT), F32),
            pltpu.VMEM((1, LAT), F32),
            pltpu.SemaphoreType.DMA((PARTS + 3,)),
        ],
        compiler_params=pltpu.CompilerParams(vmem_limit_bytes=60 << 20),
    )
    operands = (block_order, spectrum, surface_wind, wet, jnp.asarray(device_tables(devices)))
    if each == kept:
        return pl.pallas_call(
            functools.partial(pack_kernel, devices, section),
            out_shape=(shape, table_shape),
            out_specs=(vmem(), vmem()),
            **shared,
        )(*operands)
    decayed, table, tile = pl.pallas_call(
        functools.partial(loose_kernel, section),
        out_shape=(
            jax.ShapeDtypeStruct((BINS, LAT), BF),
            table_shape,
            jax.ShapeDtypeStruct((TILE, LAT), F32),
        ),
        out_specs=(vmem(), vmem(), vmem()),
        **shared,
    )(*operands)
    main = decayed[: devices * each].reshape(devices, each, LAT)
    main = jnp.pad(main, ((0, 0), (0, kept - each), (0, 0)))
    spare = decayed[devices * each :]
    spare = jnp.pad(spare, ((0, devices - spare.shape[0]), (0, 0)))[:, None]
    common = jnp.broadcast_to(tile[1:].astype(BF)[None], (devices, TILE - 1, LAT))
    return jnp.concatenate([main, spare, common], axis=1), table


def lane_whole(rows):
    return lax.broadcasted_iota(jnp.int32, (rows, LAT), 1)


def own_stress(spectrum_ref, cosines, sines, east, north):
    upper = row_ids() < TILE // 2
    along = [c * east + s * north for c, s in zip(cosines, sines)]
    totals = [jnp.zeros((TILE, LAT), F32) for _ in range(GROUP_TILES)]

    def constant(values, first, last):
        low, high = float(np.float32(values[first])), float(np.float32(values[last]))
        return low if first == last else jnp.where(upper, low, high)

    for pair in range(BINS // 16):
        both = spectrum_ref[16 * pair : 16 * pair + 16, :].astype(F32)
        for half in range(2):
            t = 2 * pair + half
            p = t % GROUP_TILES
            tile = both[TILE * half : TILE * (half + 1)]
            slope = constant(1.2 / SPEED, *tile_freqs(t))
            weight = constant(stress_coef * AREA * SIGMA / SPEED, *tile_freqs(t))
            grown = jnp.maximum(0.0, slope * along[p] - 1.0)
            totals[p] = totals[p] + (weight * tile) * grown
    return [
        jnp.sum(sum(a * b for a, b in zip(parts, totals)), axis=0, keepdims=True)
        for parts in (cosines, sines)
    ]


def spread_kernel(
    devices, section, order_ref, recv_ref, spectrum_ref, table_ref, angle_ref, out_ref,
    field_a, field_b, wet_ref, numbers_ref, slot_smem,
):
    each, kept, rows = layout(devices)
    ids = row_ids()
    lane = lax.broadcasted_iota(jnp.int32, (TILE, LAT), 1)
    unit = math.gcd(devices, UNROLL)

    def every(body, batch=1):
        if devices == unit:
            for k in range(0, unit, batch):
                body(*range(k, k + batch))
            return

        def some(block, carry):
            for k in range(0, unit, batch):
                body(*(block * unit + k + n for n in range(batch)))
            return carry

        lax.fori_loop(0, devices // unit, some, 0)

    span = min(LAT, devices)
    for block in range(devices // span):

        def place(s, tile, block=block):
            here = recv_ref[block * span + s, kept : kept + TILE, :].astype(F32)
            return jnp.where(lane == s, here, tile)

        orders = lax.fori_loop(0, span, place, jnp.zeros((TILE, LAT), F32), unroll=min(span, UNROLL))
        last = orders[TILE - 1 :].astype(jnp.int32)
        for s in range(span):
            slot_smem[(block * span + s) // section * section + last[0, s]] = block * span + s

    def weather(column):
        tile = recv_ref[column, kept : kept + TILE, :].astype(F32)
        return tile[1:2] + tile[2:3], tile[3:4] + tile[4:5], tile[5:6] + tile[6:7]

    def spread_lane(ref, t, k):
        return jnp.broadcast_to(ref[TILE * t : TILE * (t + 1), k : k + 1], (TILE, LAT))

    for t in range(rows // TILE):
        for k in range(8):
            numbers_ref[k, TILE * t : TILE * (t + 1), :] = spread_lane(table_ref, t, k)
    numbers_ref[6] = jnp.where(lane_whole(rows) == 0, 0.0, numbers_ref[6])
    numbers_ref[7] = jnp.where(lane_whole(rows) == LAT - 1, 0.0, numbers_ref[7])
    base = lax.axis_index("sec") * section
    me = base + lax.axis_index("dom")
    angles = [[spread_lane(angle_ref, p, k) for p in range(GROUP_TILES)] for k in range(2)]
    stress = own_stress(spectrum_ref, *angles, *weather(base + order_ref[0])[:2])
    column_row = jnp.full((1, LAT), order_ref[0], jnp.int32).astype(F32)
    ending = stack_rows([None, stress[0], stress[1], column_row])
    def renew(column):
        east, north, wet = weather(column)
        wet_ref[column] = jnp.broadcast_to(wet, (TILE, LAT))
        energy = recv_ref[slot_smem[column]].astype(F32)
        push = jnp.exp(jnp.maximum(0.0, numbers_ref[0] * east + numbers_ref[1] * north - numbers_ref[2]))
        field_a[column] = wet * energy * push

    every(renew)

    def around(column):
        if isinstance(column, int):
            return (column - 1) % devices, (column + 1) % devices
        return jnp.where(column == 0, devices - 1, column - 1), jnp.where(column == devices - 1, 0, column + 1)

    sure = tile_slots(devices)[1]
    northward = me < devices // 2

    def mover(source, t):
        part = pl.ds(TILE * t, TILE)
        keep, from_west, from_east, from_south, from_north = (numbers_ref[k, part, :] for k in range(3, 8))
        westerly, southerly = from_west > 0.0, from_south > 0.0
        from_x, from_y = from_west + from_east, from_south + from_north
        way = spare_way(devices) if TILE * t == kept else 0

        def shifted(here):
            if t < sure:
                return pltpu.roll(here, jnp.where(northward, 1, LAT - 1), 1)
            if way:
                return pltpu.roll(here, way % LAT, 1)
            return jnp.where(southerly, pltpu.roll(here, 1, 1), pltpu.roll(here, LAT - 1, 1))

        def moved(column):
            west, east = around(column)
            here = source[column, part, :]
            total = keep * here + from_x * jnp.where(westerly, source[west, part, :], source[east, part, :])
            return wet_ref[column] * (total + from_y * shifted(here))

        return moved

    for substep in range(SUBSTEPS - 1):
        source, target = (field_a, field_b) if substep % 2 == 0 else (field_b, field_a)
        for t in range(rows // TILE):
            moved = mover(source, t)

            def step(column):
                target[column, TILE * t : TILE * (t + 1), :] = moved(column)

            every(step)

    back = (kept + QUAD) // QUAD
    source = field_a if (SUBSTEPS - 1) % 2 == 0 else field_b
    for t in range(0, rows // TILE, 2):
        upper_tile, lower_tile = mover(source, t), mover(source, t + 1)

        def finish(*columns):
            made = []
            for column in columns:
                upper, lower = upper_tile(column), lower_tile(column)
                if TILE * (t + 1) == kept:
                    lower = jnp.where(ids == 0, lower, ending)
                made.append(jnp.concatenate([upper, lower], axis=0))
            for column, value in zip(columns, made):
                for piece in range(min(4, back - 4 * (t // 2))):
                    quarter = value[QUAD * piece : QUAD * (piece + 1)].astype(BF)
                    out_ref[slot_smem[column], 4 * (t // 2) + piece] = quarter

        every(finish, min(BATCH, unit))


def spread(devices, section, block_order, received, spectrum, table):
    each, kept, rows = layout(devices)
    span = min(LAT, devices)
    return pl.pallas_call(
        functools.partial(spread_kernel, devices, section),
        out_shape=jax.ShapeDtypeStruct((devices, (kept + QUAD) // QUAD, QUAD, LAT), BF),
        in_specs=[smem(), vmem(), vmem(), vmem(), vmem()],
        out_specs=vmem(),
        scratch_shapes=[
            pltpu.VMEM((devices, rows, LAT), F32),
            pltpu.VMEM((devices, rows, LAT), F32),
            pltpu.VMEM((devices, TILE, LAT), F32),
            pltpu.VMEM((8, rows, LAT), F32),
            pltpu.SMEM((devices,), jnp.int32),
        ],
        compiler_params=pltpu.CompilerParams(vmem_limit_bytes=32 << 20),
    )(block_order, received, spectrum, table, jnp.asarray(angle_table()))


def collect(devices, section, returned_ref, wet_ref, stress_ref):
    each, kept, rows = layout(devices)
    base = lax.axis_index("sec") * section
    rank = lax.axis_index("dom").astype(F32)

    def pick(s, total):
        tile = returned_ref[base + s, kept // QUAD].astype(F32)
        mine = jnp.broadcast_to(tile[QUAD - 1 : QUAD] == rank, (QUAD, LAT))
        return jnp.where(mine, tile, total)

    tile = lax.fori_loop(0, section, pick, jnp.zeros((QUAD, LAT), F32), unroll=8)
    stress_ref[...] = wet_ref[0:1, :] * tile[1:3]


def unpack_kernel(devices, section, returned_ref, wet_ref, out_ref, stress_ref):
    each, kept, rows = layout(devices)
    left = BINS - devices * each
    home = {t: (d, k) for d, tiles in enumerate(tile_slots(devices)[0]) for k, t in enumerate(tiles)}
    for pair in range(devices * each // 16):
        both = []
        for d, k in (home[2 * pair], home[2 * pair + 1]):
            both += [returned_ref[d, 2 * k + half].astype(F32) for half in range(2)]
        out_ref[16 * pair : 16 * (pair + 1), :] = jnp.concatenate(both, axis=0).astype(BF)
    spare = []
    for tile in range(left // TILE):
        heads = [returned_ref[TILE * tile + r, kept // QUAD].astype(F32)[:1] for r in range(TILE)]
        spare.append(stack_rows(heads))
    out_ref[devices * each :, :] = jnp.concatenate(spare, axis=0).astype(BF)
    collect(devices, section, returned_ref, wet_ref, stress_ref)


def unpacked(devices, section, returned, wet):
    each, kept, rows = layout(devices)
    left = BINS - devices * each
    stress_shape = jax.ShapeDtypeStruct((2, LAT), F32)
    params = pltpu.CompilerParams(vmem_limit_bytes=24 << 20)
    if each == kept and devices % 2 == 0 and each % TILE == 0 and left % 16 == 0:
        return pl.pallas_call(
            functools.partial(unpack_kernel, devices, section),
            out_shape=(jax.ShapeDtypeStruct((BINS, LAT), BF), stress_shape),
            in_specs=[vmem(), vmem()],
            out_specs=(vmem(), vmem()),
            compiler_params=params,
        )(returned, wet)
    stress = pl.pallas_call(
        functools.partial(collect, devices, section),
        out_shape=stress_shape,
        in_specs=[vmem(), vmem()],
        out_specs=vmem(),
        compiler_params=params,
    )(returned, wet)
    returned = returned.reshape(devices, -1, LAT)
    main = returned[:, :each].reshape(devices * each, LAT)
    return jnp.concatenate([main, returned[:left, kept]], axis=0), stress


def on_device(devices, section, spectrum, surface_wind, wet_mask, block_order):
    wet = wet_mask.reshape(1, LAT)
    sending, table = packed(devices, section, block_order, spectrum, surface_wind, wet)
    received = lax.all_to_all(sending, AXES, split_axis=0, concat_axis=0, tiled=True)
    leaving = spread(devices, section, block_order, received, spectrum, table)
    returned = lax.all_to_all(leaving, AXES, split_axis=0, concat_axis=0, tiled=True)
    return unpacked(devices, section, returned, wet)


def solution(mesh):
    section = mesh.shape["dom"]
    devices = mesh.shape["sec"] * section
    placed = (P(None, AXES), P(None, AXES), P(AXES), P(AXES))
    return jax.shard_map(
        functools.partial(on_device, devices, section),
        mesh=mesh,
        in_specs=placed,
        out_specs=(P(None, AXES), P(None, AXES)),
        check_vma=False,
    )
```

```python
import functools
import math

import jax
import jax.numpy as jnp
import numpy as np
from jax import lax
from jax.experimental import pallas as pl
from jax.experimental.pallas import tpu as pltpu
from jax.sharding import PartitionSpec as P

NF = 36
ND = 36
BINS = NF * ND
LAT = 128
SUBSTEPS = 4

gravity = 9.81
base_freq = 0.035
freq_growth = 1.1
wind_rate = 0.015
dissip_rate = 0.008
steep_ref = 3.0
stress_coef = 0.01
courant = 0.62

AXES = ("sec", "dom")
TILE = 8
QUAD = 4
UNROLL = 32
BATCH = 8
PART = 144
PARTS = BINS // PART
GROUP_TILES = 9
BF = jnp.bfloat16
F32 = jnp.float32

FREQ = np.arange(NF, dtype=np.float64)
SIGMA = 2.0 * math.pi * base_freq * freq_growth**FREQ
WAVENUM = SIGMA * SIGMA / gravity
SPEED = gravity / SIGMA
AREA = 0.1 * SIGMA * (2.0 * math.pi / ND)
THETA = 2.0 * math.pi * np.arange(ND, dtype=np.float64) / ND
COS, SIN = (np.where(np.abs(wave) < 1e-9, 0.0, wave) for wave in (np.cos(THETA), np.sin(THETA)))


def vmem():
    return pl.BlockSpec(memory_space=pltpu.VMEM)


def smem():
    return pl.BlockSpec(memory_space=pltpu.SMEM)


def hbm():
    return pl.BlockSpec(memory_space=pltpu.HBM)


def layout(devices):
    each = BINS // devices
    rows = -(-(each + TILE) // 16) * 16
    return each, rows - TILE, rows


def tile_slots(devices):
    each, kept, rows = layout(devices)
    if each != kept:
        return None, 0
    count, half = each // TILE, devices // 2
    ways = [[], [], []]
    for t in range(devices * count):
        wave = SIN[(TILE * t + np.arange(TILE)) % ND]
        ways[0 if (wave >= 0).all() else 1 if (wave <= 0).all() else 2].append(t)
    sure = min(len(ways[0]) // half, len(ways[1]) // half, count)
    rest = sorted(ways[0][sure * half :] + ways[1][sure * half :] + ways[2])
    slots = []
    for d in range(devices):
        way, place = ways[d // half], d % half
        mixed = rest[(count - sure) * d : (count - sure) * (d + 1)]
        slots.append(way[sure * place : sure * (place + 1)] + mixed)
    return slots, sure


def spare_way(devices):
    wave = SIN[np.arange(BINS // devices * devices, BINS) % ND]
    return 1 if (wave >= 0).all() else -1 if (wave <= 0).all() else 0


def device_tables(devices):
    each, kept, rows = layout(devices)
    slots = tile_slots(devices)[0]
    table = np.zeros((devices, rows, LAT), np.float64)
    for device in range(devices):
        bins = np.full((rows,), -1)
        if slots is None:
            bins[:each] = device * each + np.arange(each)
        else:
            bins[:each] = (TILE * np.array(slots[device])[:, None] + np.arange(TILE)).reshape(-1)
        if devices * each + device < BINS:
            bins[kept] = devices * each + device
        real = bins >= 0
        i, j = np.maximum(bins, 0) // ND, np.maximum(bins, 0) % ND
        scale = wind_rate * SIGMA[i]
        travel = courant * freq_growth ** (-i.astype(np.float64))
        cx, cy = travel * COS[j], travel * SIN[j]
        values = (
            scale * 1.2 / SPEED[i] * COS[j],
            scale * 1.2 / SPEED[i] * SIN[j],
            scale,
            1.0 - np.abs(cx) - np.abs(cy),
            np.maximum(cx, 0.0),
            np.maximum(-cx, 0.0),
            np.maximum(cy, 0.0),
            np.maximum(-cy, 0.0),
        )
        for lane, value in enumerate(values):
            table[device, :, lane] = np.where(real, value, 0.0)
    return table.astype(np.float32)


def angle_table():
    table = np.zeros((GROUP_TILES * TILE, LAT), np.float64)
    angle = np.arange(GROUP_TILES * TILE) % ND
    table[:, 0], table[:, 1] = COS[angle], SIN[angle]
    return table.astype(np.float32)


def split(value):
    high = value.astype(BF)
    return high.astype(F32), (value - high.astype(F32)).astype(BF).astype(F32)


def row_ids():
    return lax.broadcasted_iota(jnp.int32, (TILE, LAT), 0)


def stack_rows(rows):
    ids = row_ids()
    tile = jnp.zeros((TILE, LAT), F32)
    for r, row in enumerate(rows):
        if row is not None:
            tile = jnp.where(ids == r, jnp.broadcast_to(row, (TILE, LAT)), tile)
    return tile


def tile_freqs(t):
    return (TILE * t) // ND, (TILE * t + TILE - 1) // ND


def decayed_tiles(spectrum_ref, arrive):
    ids = row_ids()
    upper = ids < TILE // 2
    tiles = []
    sums = [jnp.zeros((TILE, LAT), F32) for _ in range(3)]
    for group in range(NF // 2):
        if group % 2 == 0:
            arrive(group // 2)
            for pair in range(GROUP_TILES):
                first = PART * (group // 2) + 16 * pair
                both = spectrum_ref[first : first + 16, :].astype(F32)
                tiles += [both[:TILE], both[TILE:]]
        nine = tiles[GROUP_TILES * group : GROUP_TILES * (group + 1)]
        low = (nine[0] + nine[1]) + (nine[2] + nine[3]) + jnp.where(upper, nine[4], 0.0)
        high = (nine[5] + nine[6]) + (nine[7] + nine[8]) + jnp.where(upper, 0.0, nine[4])
        for i, part in ((2 * group, low), (2 * group + 1, high)):
            weights = (AREA[i], AREA[i] / SIGMA[i], AREA[i] / math.sqrt(WAVENUM[i]))
            sums = [s + float(np.float32(w)) * part for s, w in zip(sums, weights)]
    moments = [jnp.broadcast_to(jnp.sum(s, axis=0, keepdims=True), (TILE, LAT)) for s in sums]
    mean_freq = moments[0] / moments[1]
    mean_wavenum = (moments[0] / moments[2]) ** 2
    steepness = moments[0] * mean_wavenum * mean_wavenum
    strength = mean_freq * (steepness / steep_ref) ** 2
    inverse = 1.0 / mean_wavenum
    factors = []
    for i in range(NF):
        ratio = float(np.float32(WAVENUM[i])) * inverse
        factors.append(jnp.exp(-dissip_rate * (strength * (0.5 * ratio + 0.5 * ratio * ratio))))

    def decayed(t):
        first, last = tile_freqs(t)
        factor = factors[first]
        if last != first:
            factor = jnp.where(upper, factor, factors[last])
        return spectrum_ref[TILE * t : TILE * (t + 1), :].astype(F32) * factor

    return decayed


def shared_tile(wind_ref, wet_ref, order):
    east, north, wet = split(wind_ref[0:1, :]), split(wind_ref[1:2, :]), split(wet_ref[0:1, :])
    column = jnp.full((1, LAT), order, jnp.int32).astype(F32)
    return stack_rows([None, *east, *north, *wet, column])


def fetch(section, spectrum_hbm, wind_hbm, wet_hbm, tables_hbm, spectrum_ref, wind_ref, wet_ref, table_ref, sems):
    me = lax.axis_index("sec") * section + lax.axis_index("dom")
    parts = [
        pltpu.make_async_copy(
            spectrum_hbm.at[pl.ds(PART * k, PART), :], spectrum_ref.at[pl.ds(PART * k, PART), :], sems.at[k]
        )
        for k in range(PARTS)
    ]
    rest = [
        pltpu.make_async_copy(source, target, sems.at[PARTS + k])
        for k, (source, target) in enumerate(
            ((wind_hbm, wind_ref), (wet_hbm, wet_ref), (tables_hbm.at[me], table_ref))
        )
    ]
    for copy in parts + rest:
        copy.start()

    def arrive(part):
        parts[part].wait()

    def arrive_rest():
        for copy in rest:
            copy.wait()

    return arrive, arrive_rest


def pack_kernel(
    devices, section, order_ref, spectrum_hbm, wind_hbm, wet_hbm, tables_hbm, out_ref, table_ref,
    spectrum_ref, wind_ref, wet_ref, sems,
):
    each, kept, rows = layout(devices)
    arrive, arrive_rest = fetch(
        section, spectrum_hbm, wind_hbm, wet_hbm, tables_hbm, spectrum_ref, wind_ref, wet_ref, table_ref, sems
    )
    decayed = decayed_tiles(spectrum_ref, arrive)
    arrive_rest()
    shared = shared_tile(wind_ref, wet_ref, order_ref[0])
    first = row_ids() == 0
    left = BINS - devices * each
    slots = tile_slots(devices)[0]
    spares = [decayed(t) for t in range(devices * each // TILE, BINS // TILE)]
    for d in range(devices):
        last = shared
        if d < left:
            row = spares[d // TILE][d % TILE : d % TILE + 1]
            last = jnp.where(first, jnp.broadcast_to(row, (TILE, LAT)), shared)
        chunk = jnp.concatenate([decayed(t) for t in slots[d]] + [last], axis=0)
        out_ref[d] = chunk.astype(BF)


def loose_kernel(
    section, order_ref, spectrum_hbm, wind_hbm, wet_hbm, tables_hbm, out_ref, table_ref, shared_ref,
    spectrum_ref, wind_ref, wet_ref, sems,
):
    arrive, arrive_rest = fetch(
        section, spectrum_hbm, wind_hbm, wet_hbm, tables_hbm, spectrum_ref, wind_ref, wet_ref, table_ref, sems
    )
    decayed = decayed_tiles(spectrum_ref, arrive)
    arrive_rest()
    for pair in range(BINS // 16):
        both = jnp.concatenate([decayed(2 * pair), decayed(2 * pair + 1)], axis=0)
        out_ref[16 * pair : 16 * pair + 16, :] = both.astype(BF)
    shared_ref[...] = shared_tile(wind_ref, wet_ref, order_ref[0])


def packed(devices, section, block_order, spectrum, surface_wind, wet):
    each, kept, rows = layout(devices)
    shape = jax.ShapeDtypeStruct((devices, rows, LAT), BF)
    table_shape = jax.ShapeDtypeStruct((rows, LAT), F32)
    shared = dict(
        in_specs=[smem(), hbm(), hbm(), hbm(), hbm()],
        scratch_shapes=[
            pltpu.VMEM((BINS, LAT), BF),
            pltpu.VMEM((2, LAT), F32),
            pltpu.VMEM((1, LAT), F32),
            pltpu.SemaphoreType.DMA((PARTS + 3,)),
        ],
        compiler_params=pltpu.CompilerParams(vmem_limit_bytes=24 << 20),
    )
    stay = (spectrum, surface_wind, wet, jnp.asarray(device_tables(devices)))
    operands = (block_order, *(pltpu.with_memory_space_constraint(array, pltpu.HBM) for array in stay))
    if each == kept:
        return pl.pallas_call(
            functools.partial(pack_kernel, devices, section),
            out_shape=(shape, table_shape),
            out_specs=(vmem(), vmem()),
            **shared,
        )(*operands)
    decayed, table, tile = pl.pallas_call(
        functools.partial(loose_kernel, section),
        out_shape=(
            jax.ShapeDtypeStruct((BINS, LAT), BF),
            table_shape,
            jax.ShapeDtypeStruct((TILE, LAT), F32),
        ),
        out_specs=(vmem(), vmem(), vmem()),
        **shared,
    )(*operands)
    main = decayed[: devices * each].reshape(devices, each, LAT)
    main = jnp.pad(main, ((0, 0), (0, kept - each), (0, 0)))
    spare = decayed[devices * each :]
    spare = jnp.pad(spare, ((0, devices - spare.shape[0]), (0, 0)))[:, None]
    common = jnp.broadcast_to(tile[1:].astype(BF)[None], (devices, TILE - 1, LAT))
    return jnp.concatenate([main, spare, common], axis=1), table


def lane_whole(rows):
    return lax.broadcasted_iota(jnp.int32, (rows, LAT), 1)


def own_stress(spectrum_ref, cosines, sines, east, north):
    upper = row_ids() < TILE // 2
    along = [c * east + s * north for c, s in zip(cosines, sines)]
    totals = [jnp.zeros((TILE, LAT), F32) for _ in range(GROUP_TILES)]

    def constant(values, first, last):
        low, high = float(np.float32(values[first])), float(np.float32(values[last]))
        return low if first == last else jnp.where(upper, low, high)

    for pair in range(BINS // 16):
        both = spectrum_ref[16 * pair : 16 * pair + 16, :].astype(F32)
        for half in range(2):
            t = 2 * pair + half
            p = t % GROUP_TILES
            tile = both[TILE * half : TILE * (half + 1)]
            slope = constant(1.2 / SPEED, *tile_freqs(t))
            weight = constant(stress_coef * AREA * SIGMA / SPEED, *tile_freqs(t))
            grown = jnp.maximum(0.0, slope * along[p] - 1.0)
            totals[p] = totals[p] + (weight * tile) * grown
    return [
        jnp.sum(sum(a * b for a, b in zip(parts, totals)), axis=0, keepdims=True)
        for parts in (cosines, sines)
    ]


def spread_kernel(
    devices, section, order_ref, recv_ref, spectrum_ref, table_ref, angle_ref, out_ref,
    field_a, field_b, wet_ref, numbers_ref, slot_smem,
):
    each, kept, rows = layout(devices)
    ids = row_ids()
    lane = lax.broadcasted_iota(jnp.int32, (TILE, LAT), 1)
    unit = math.gcd(devices, UNROLL)

    def every(body, batch=1):
        if devices == unit:
            for k in range(0, unit, batch):
                body(*range(k, k + batch))
            return

        def some(block, carry):
            for k in range(0, unit, batch):
                body(*(block * unit + k + n for n in range(batch)))
            return carry

        lax.fori_loop(0, devices // unit, some, 0)

    span = min(LAT, devices)
    for block in range(devices // span):

        def place(s, tile, block=block):
            here = recv_ref[block * span + s, kept : kept + TILE, :].astype(F32)
            return jnp.where(lane == s, here, tile)

        orders = lax.fori_loop(0, span, place, jnp.zeros((TILE, LAT), F32), unroll=min(span, UNROLL))
        last = orders[TILE - 1 :].astype(jnp.int32)
        for s in range(span):
            slot_smem[(block * span + s) // section * section + last[0, s]] = block * span + s

    def weather(column):
        tile = recv_ref[column, kept : kept + TILE, :].astype(F32)
        return tile[1:2] + tile[2:3], tile[3:4] + tile[4:5], tile[5:6] + tile[6:7]

    def spread_lane(ref, t, k):
        return jnp.broadcast_to(ref[TILE * t : TILE * (t + 1), k : k + 1], (TILE, LAT))

    for t in range(rows // TILE):
        for k in range(8):
            numbers_ref[k, TILE * t : TILE * (t + 1), :] = spread_lane(table_ref, t, k)
    numbers_ref[6] = jnp.where(lane_whole(rows) == 0, 0.0, numbers_ref[6])
    numbers_ref[7] = jnp.where(lane_whole(rows) == LAT - 1, 0.0, numbers_ref[7])
    base = lax.axis_index("sec") * section
    me = base + lax.axis_index("dom")
    angles = [[spread_lane(angle_ref, p, k) for p in range(GROUP_TILES)] for k in range(2)]
    stress = own_stress(spectrum_ref, *angles, *weather(base + order_ref[0])[:2])
    column_row = jnp.full((1, LAT), order_ref[0], jnp.int32).astype(F32)
    ending = stack_rows([None, stress[0], stress[1], column_row])
    def renew(column):
        east, north, wet = weather(column)
        wet_ref[column] = jnp.broadcast_to(wet, (TILE, LAT))
        energy = recv_ref[slot_smem[column]].astype(F32)
        push = jnp.exp(jnp.maximum(0.0, numbers_ref[0] * east + numbers_ref[1] * north - numbers_ref[2]))
        field_a[column] = wet * energy * push

    every(renew)

    def around(column):
        if isinstance(column, int):
            return (column - 1) % devices, (column + 1) % devices
        return jnp.where(column == 0, devices - 1, column - 1), jnp.where(column == devices - 1, 0, column + 1)

    sure = tile_slots(devices)[1]
    northward = me < devices // 2

    def mover(source, t):
        part = pl.ds(TILE * t, TILE)
        keep, from_west, from_east, from_south, from_north = (numbers_ref[k, part, :] for k in range(3, 8))
        westerly, southerly = from_west > 0.0, from_south > 0.0
        from_x, from_y = from_west + from_east, from_south + from_north
        way = spare_way(devices) if TILE * t == kept else 0

        def shifted(here):
            if t < sure:
                return pltpu.roll(here, jnp.where(northward, 1, LAT - 1), 1)
            if way:
                return pltpu.roll(here, way % LAT, 1)
            return jnp.where(southerly, pltpu.roll(here, 1, 1), pltpu.roll(here, LAT - 1, 1))

        def moved(column):
            west, east = around(column)
            here = source[column, part, :]
            total = keep * here + from_x * jnp.where(westerly, source[west, part, :], source[east, part, :])
            return wet_ref[column] * (total + from_y * shifted(here))

        return moved

    for substep in range(SUBSTEPS - 1):
        source, target = (field_a, field_b) if substep % 2 == 0 else (field_b, field_a)
        for t in range(rows // TILE):
            moved = mover(source, t)

            def step(column):
                target[column, TILE * t : TILE * (t + 1), :] = moved(column)

            every(step)

    back = (kept + QUAD) // QUAD
    source = field_a if (SUBSTEPS - 1) % 2 == 0 else field_b
    for t in range(0, rows // TILE, 2):
        upper_tile, lower_tile = mover(source, t), mover(source, t + 1)

        def finish(*columns):
            made = []
            for column in columns:
                upper, lower = upper_tile(column), lower_tile(column)
                if TILE * (t + 1) == kept:
                    lower = jnp.where(ids == 0, lower, ending)
                made.append(jnp.concatenate([upper, lower], axis=0))
            for column, value in zip(columns, made):
                for piece in range(min(4, back - 4 * (t // 2))):
                    quarter = value[QUAD * piece : QUAD * (piece + 1)].astype(BF)
                    out_ref[slot_smem[column], 4 * (t // 2) + piece] = quarter

        every(finish, min(BATCH, unit))


def spread(devices, section, block_order, received, spectrum, table):
    each, kept, rows = layout(devices)
    span = min(LAT, devices)
    return pl.pallas_call(
        functools.partial(spread_kernel, devices, section),
        out_shape=jax.ShapeDtypeStruct((devices, (kept + QUAD) // QUAD, QUAD, LAT), BF),
        in_specs=[smem(), vmem(), vmem(), vmem(), vmem()],
        out_specs=vmem(),
        scratch_shapes=[
            pltpu.VMEM((devices, rows, LAT), F32),
            pltpu.VMEM((devices, rows, LAT), F32),
            pltpu.VMEM((devices, TILE, LAT), F32),
            pltpu.VMEM((8, rows, LAT), F32),
            pltpu.SMEM((devices,), jnp.int32),
        ],
        compiler_params=pltpu.CompilerParams(vmem_limit_bytes=32 << 20),
    )(block_order, received, spectrum, table, jnp.asarray(angle_table()))


def collect(devices, section, returned_ref, wet_ref, stress_ref):
    each, kept, rows = layout(devices)
    base = lax.axis_index("sec") * section
    rank = lax.axis_index("dom").astype(F32)

    def pick(s, total):
        tile = returned_ref[base + s, kept // QUAD].astype(F32)
        mine = jnp.broadcast_to(tile[QUAD - 1 : QUAD] == rank, (QUAD, LAT))
        return jnp.where(mine, tile, total)

    tile = lax.fori_loop(0, section, pick, jnp.zeros((QUAD, LAT), F32), unroll=8)
    stress_ref[...] = wet_ref[0:1, :] * tile[1:3]


def unpack_kernel(devices, section, returned_ref, wet_ref, out_ref, stress_ref):
    each, kept, rows = layout(devices)
    left = BINS - devices * each
    home = {t: (d, k) for d, tiles in enumerate(tile_slots(devices)[0]) for k, t in enumerate(tiles)}
    for pair in range(devices * each // 16):
        both = []
        for d, k in (home[2 * pair], home[2 * pair + 1]):
            both += [returned_ref[d, 2 * k + half].astype(F32) for half in range(2)]
        out_ref[16 * pair : 16 * (pair + 1), :] = jnp.concatenate(both, axis=0).astype(BF)
    spare = []
    for tile in range(left // TILE):
        heads = [returned_ref[TILE * tile + r, kept // QUAD].astype(F32)[:1] for r in range(TILE)]
        spare.append(stack_rows(heads))
    out_ref[devices * each :, :] = jnp.concatenate(spare, axis=0).astype(BF)
    collect(devices, section, returned_ref, wet_ref, stress_ref)


def unpacked(devices, section, returned, wet):
    each, kept, rows = layout(devices)
    left = BINS - devices * each
    stress_shape = jax.ShapeDtypeStruct((2, LAT), F32)
    params = pltpu.CompilerParams(vmem_limit_bytes=24 << 20)
    if each == kept and devices % 2 == 0 and each % TILE == 0 and left % 16 == 0:
        return pl.pallas_call(
            functools.partial(unpack_kernel, devices, section),
            out_shape=(jax.ShapeDtypeStruct((BINS, LAT), BF), stress_shape),
            in_specs=[vmem(), vmem()],
            out_specs=(vmem(), vmem()),
            compiler_params=params,
        )(returned, wet)
    stress = pl.pallas_call(
        functools.partial(collect, devices, section),
        out_shape=stress_shape,
        in_specs=[vmem(), vmem()],
        out_specs=vmem(),
        compiler_params=params,
    )(returned, wet)
    returned = returned.reshape(devices, -1, LAT)
    main = returned[:, :each].reshape(devices * each, LAT)
    return jnp.concatenate([main, returned[:left, kept]], axis=0), stress


def on_device(devices, section, spectrum, surface_wind, wet_mask, block_order):
    wet = wet_mask.reshape(1, LAT)
    sending, table = packed(devices, section, block_order, spectrum, surface_wind, wet)
    received = lax.all_to_all(sending, AXES, split_axis=0, concat_axis=0, tiled=True)
    leaving = spread(devices, section, block_order, received, spectrum, table)
    returned = lax.all_to_all(leaving, AXES, split_axis=0, concat_axis=0, tiled=True)
    return unpacked(devices, section, returned, wet)


def solution(mesh):
    section = mesh.shape["dom"]
    devices = mesh.shape["sec"] * section
    placed = (P(None, AXES), P(None, AXES), P(AXES), P(AXES))
    return jax.shard_map(
        functools.partial(on_device, devices, section),
        mesh=mesh,
        in_specs=placed,
        out_specs=(P(None, AXES), P(None, AXES)),
        check_vma=False,
    )
```

```python
import functools
import math

import jax
import jax.numpy as jnp
import numpy as np
from jax import lax
from jax.experimental import pallas as pl
from jax.experimental.pallas import tpu as pltpu
from jax.sharding import PartitionSpec as P

NF = 36
ND = 36
BINS = NF * ND
LAT = 128
SUBSTEPS = 4

gravity = 9.81
base_freq = 0.035
freq_growth = 1.1
wind_rate = 0.015
dissip_rate = 0.008
steep_ref = 3.0
stress_coef = 0.01
courant = 0.62

AXES = ("sec", "dom")
TILE = 8
QUAD = 4
UNROLL = 32
BATCH = 8
PART = 144
PARTS = BINS // PART
GROUP_TILES = 9
BF = jnp.bfloat16
F32 = jnp.float32

FREQ = np.arange(NF, dtype=np.float64)
SIGMA = 2.0 * math.pi * base_freq * freq_growth**FREQ
WAVENUM = SIGMA * SIGMA / gravity
SPEED = gravity / SIGMA
AREA = 0.1 * SIGMA * (2.0 * math.pi / ND)
THETA = 2.0 * math.pi * np.arange(ND, dtype=np.float64) / ND
COS, SIN = (np.where(np.abs(wave) < 1e-9, 0.0, wave) for wave in (np.cos(THETA), np.sin(THETA)))


def vmem():
    return pl.BlockSpec(memory_space=pltpu.VMEM)


def smem():
    return pl.BlockSpec(memory_space=pltpu.SMEM)


def hbm():
    return pl.BlockSpec(memory_space=pltpu.HBM)


def layout(devices):
    each = BINS // devices
    rows = -(-(each + TILE) // 16) * 16
    return each, rows - TILE, rows


def tile_slots(devices):
    each, kept, rows = layout(devices)
    if each != kept:
        return None, 0
    count, half = each // TILE, devices // 2
    ways = [[], [], []]
    for t in range(devices * count):
        wave = SIN[(TILE * t + np.arange(TILE)) % ND]
        ways[0 if (wave >= 0).all() else 1 if (wave <= 0).all() else 2].append(t)
    def eastward(t):
        return (COS[(TILE * t + np.arange(TILE)) % ND] >= 0).all()

    def westward(t):
        return (COS[(TILE * t + np.arange(TILE)) % ND] <= 0).all()

    ways[0].sort(key=lambda t: (not eastward(t), t))
    ways[1].sort(key=lambda t: (not eastward(t), t))
    sure = min(len(ways[0]) // half, len(ways[1]) // half, count)
    rest = sorted(ways[0][sure * half :] + ways[1][sure * half :] + ways[2], key=lambda t: (not westward(t), t))
    slots = []
    for d in range(devices):
        way, place = ways[d // half], d % half
        slots.append([way[half * k + place] for k in range(sure)] + [rest[devices * k + d] for k in range(count - sure)])
    return slots, sure


def column_way(devices, k):
    slots = tile_slots(devices)[0]
    if slots is None or k >= len(slots[0]):
        return 0
    wave = np.concatenate([COS[(TILE * tiles[k] + np.arange(TILE)) % ND] for tiles in slots])
    return 1 if (wave >= 0).all() else -1 if (wave <= 0).all() else 0


def spare_way(devices):
    wave = SIN[np.arange(BINS // devices * devices, BINS) % ND]
    return 1 if (wave >= 0).all() else -1 if (wave <= 0).all() else 0


def device_tables(devices):
    each, kept, rows = layout(devices)
    slots = tile_slots(devices)[0]
    table = np.zeros((devices, rows, LAT), np.float64)
    for device in range(devices):
        bins = np.full((rows,), -1)
        if slots is None:
            bins[:each] = device * each + np.arange(each)
        else:
            bins[:each] = (TILE * np.array(slots[device])[:, None] + np.arange(TILE)).reshape(-1)
        if devices * each + device < BINS:
            bins[kept] = devices * each + device
        real = bins >= 0
        i, j = np.maximum(bins, 0) // ND, np.maximum(bins, 0) % ND
        scale = wind_rate * SIGMA[i]
        travel = courant * freq_growth ** (-i.astype(np.float64))
        cx, cy = travel * COS[j], travel * SIN[j]
        values = (
            scale * 1.2 / SPEED[i] * COS[j],
            scale * 1.2 / SPEED[i] * SIN[j],
            scale,
            1.0 - np.abs(cx) - np.abs(cy),
            np.maximum(cx, 0.0),
            np.maximum(-cx, 0.0),
            np.maximum(cy, 0.0),
            np.maximum(-cy, 0.0),
        )
        for lane, value in enumerate(values):
            table[device, :, lane] = np.where(real, value, 0.0)
    return table.astype(np.float32)


def angle_table():
    table = np.zeros((GROUP_TILES * TILE, LAT), np.float64)
    angle = np.arange(GROUP_TILES * TILE) % ND
    table[:, 0], table[:, 1] = COS[angle], SIN[angle]
    return table.astype(np.float32)


def split(value):
    high = value.astype(BF)
    return high.astype(F32), (value - high.astype(F32)).astype(BF).astype(F32)


def row_ids():
    return lax.broadcasted_iota(jnp.int32, (TILE, LAT), 0)


def stack_rows(rows):
    ids = row_ids()
    tile = jnp.zeros((TILE, LAT), F32)
    for r, row in enumerate(rows):
        if row is not None:
            tile = jnp.where(ids == r, jnp.broadcast_to(row, (TILE, LAT)), tile)
    return tile


def tile_freqs(t):
    return (TILE * t) // ND, (TILE * t + TILE - 1) // ND


def decayed_tiles(spectrum_ref, arrive):
    ids = row_ids()
    upper = ids < TILE // 2
    tiles = []
    sums = [jnp.zeros((TILE, LAT), F32) for _ in range(3)]
    for group in range(NF // 2):
        if group % 2 == 0:
            arrive(group // 2)
            for pair in range(GROUP_TILES):
                first = PART * (group // 2) + 16 * pair
                both = spectrum_ref[first : first + 16, :].astype(F32)
                tiles += [both[:TILE], both[TILE:]]
        nine = tiles[GROUP_TILES * group : GROUP_TILES * (group + 1)]
        low = (nine[0] + nine[1]) + (nine[2] + nine[3]) + jnp.where(upper, nine[4], 0.0)
        high = (nine[5] + nine[6]) + (nine[7] + nine[8]) + jnp.where(upper, 0.0, nine[4])
        for i, part in ((2 * group, low), (2 * group + 1, high)):
            weights = (AREA[i], AREA[i] / SIGMA[i], AREA[i] / math.sqrt(WAVENUM[i]))
            sums = [s + float(np.float32(w)) * part for s, w in zip(sums, weights)]
    moments = [jnp.broadcast_to(jnp.sum(s, axis=0, keepdims=True), (TILE, LAT)) for s in sums]
    mean_freq = moments[0] / moments[1]
    mean_wavenum = (moments[0] / moments[2]) ** 2
    steepness = moments[0] * mean_wavenum * mean_wavenum
    strength = mean_freq * (steepness / steep_ref) ** 2
    inverse = 1.0 / mean_wavenum
    factors = []
    for i in range(NF):
        ratio = float(np.float32(WAVENUM[i])) * inverse
        factors.append(jnp.exp(-dissip_rate * (strength * (0.5 * ratio + 0.5 * ratio * ratio))))

    def decayed(t):
        first, last = tile_freqs(t)
        factor = factors[first]
        if last != first:
            factor = jnp.where(upper, factor, factors[last])
        return spectrum_ref[TILE * t : TILE * (t + 1), :].astype(F32) * factor

    return decayed


def shared_tile(wind_ref, wet_ref, order):
    east, north, wet = split(wind_ref[0:1, :]), split(wind_ref[1:2, :]), split(wet_ref[0:1, :])
    column = jnp.full((1, LAT), order, jnp.int32).astype(F32)
    return stack_rows([None, *east, *north, *wet, column])


def fetch(section, spectrum_hbm, wind_hbm, wet_hbm, tables_hbm, spectrum_ref, wind_ref, wet_ref, table_ref, sems):
    me = lax.axis_index("sec") * section + lax.axis_index("dom")
    parts = [
        pltpu.make_async_copy(
            spectrum_hbm.at[pl.ds(PART * k, PART), :], spectrum_ref.at[pl.ds(PART * k, PART), :], sems.at[k]
        )
        for k in range(PARTS)
    ]
    rest = [
        pltpu.make_async_copy(source, target, sems.at[PARTS + k])
        for k, (source, target) in enumerate(
            ((wind_hbm, wind_ref), (wet_hbm, wet_ref), (tables_hbm.at[me], table_ref))
        )
    ]
    for copy in parts + rest:
        copy.start()

    def arrive(part):
        parts[part].wait()

    def arrive_rest():
        for copy in rest:
            copy.wait()

    return arrive, arrive_rest


def pack_kernel(
    devices, section, order_ref, spectrum_hbm, wind_hbm, wet_hbm, tables_hbm, out_ref, table_ref,
    spectrum_ref, wind_ref, wet_ref, sems,
):
    each, kept, rows = layout(devices)
    arrive, arrive_rest = fetch(
        section, spectrum_hbm, wind_hbm, wet_hbm, tables_hbm, spectrum_ref, wind_ref, wet_ref, table_ref, sems
    )
    decayed = decayed_tiles(spectrum_ref, arrive)
    arrive_rest()
    shared = shared_tile(wind_ref, wet_ref, order_ref[0])
    first = row_ids() == 0
    left = BINS - devices * each
    slots = tile_slots(devices)[0]
    spares = [decayed(t) for t in range(devices * each // TILE, BINS // TILE)]
    for d in range(devices):
        last = shared
        if d < left:
            row = spares[d // TILE][d % TILE : d % TILE + 1]
            last = jnp.where(first, jnp.broadcast_to(row, (TILE, LAT)), shared)
        chunk = jnp.concatenate([decayed(t) for t in slots[d]] + [last], axis=0)
        out_ref[d] = chunk.astype(BF)


def loose_kernel(
    section, order_ref, spectrum_hbm, wind_hbm, wet_hbm, tables_hbm, out_ref, table_ref, shared_ref,
    spectrum_ref, wind_ref, wet_ref, sems,
):
    arrive, arrive_rest = fetch(
        section, spectrum_hbm, wind_hbm, wet_hbm, tables_hbm, spectrum_ref, wind_ref, wet_ref, table_ref, sems
    )
    decayed = decayed_tiles(spectrum_ref, arrive)
    arrive_rest()
    for pair in range(BINS // 16):
        both = jnp.concatenate([decayed(2 * pair), decayed(2 * pair + 1)], axis=0)
        out_ref[16 * pair : 16 * pair + 16, :] = both.astype(BF)
    shared_ref[...] = shared_tile(wind_ref, wet_ref, order_ref[0])


def packed(devices, section, block_order, spectrum, surface_wind, wet):
    each, kept, rows = layout(devices)
    shape = jax.ShapeDtypeStruct((devices, rows, LAT), BF)
    table_shape = jax.ShapeDtypeStruct((rows, LAT), F32)
    shared = dict(
        in_specs=[smem(), hbm(), hbm(), hbm(), hbm()],
        scratch_shapes=[
            pltpu.VMEM((BINS, LAT), BF),
            pltpu.VMEM((2, LAT), F32),
            pltpu.VMEM((1, LAT), F32),
            pltpu.SemaphoreType.DMA((PARTS + 3,)),
        ],
        compiler_params=pltpu.CompilerParams(vmem_limit_bytes=24 << 20),
    )
    stay = (spectrum, surface_wind, wet, jnp.asarray(device_tables(devices)))
    operands = (block_order, *(pltpu.with_memory_space_constraint(array, pltpu.HBM) for array in stay))
    if each == kept:
        return pl.pallas_call(
            functools.partial(pack_kernel, devices, section),
            out_shape=(shape, table_shape),
            out_specs=(vmem(), vmem()),
            **shared,
        )(*operands)
    decayed, table, tile = pl.pallas_call(
        functools.partial(loose_kernel, section),
        out_shape=(
            jax.ShapeDtypeStruct((BINS, LAT), BF),
            table_shape,
            jax.ShapeDtypeStruct((TILE, LAT), F32),
        ),
        out_specs=(vmem(), vmem(), vmem()),
        **shared,
    )(*operands)
    main = decayed[: devices * each].reshape(devices, each, LAT)
    main = jnp.pad(main, ((0, 0), (0, kept - each), (0, 0)))
    spare = decayed[devices * each :]
    spare = jnp.pad(spare, ((0, devices - spare.shape[0]), (0, 0)))[:, None]
    common = jnp.broadcast_to(tile[1:].astype(BF)[None], (devices, TILE - 1, LAT))
    return jnp.concatenate([main, spare, common], axis=1), table


def lane_whole(rows):
    return lax.broadcasted_iota(jnp.int32, (rows, LAT), 1)


def own_stress(spectrum_ref, cosines, sines, east, north):
    upper = row_ids() < TILE // 2
    along = [c * east + s * north for c, s in zip(cosines, sines)]
    totals = [jnp.zeros((TILE, LAT), F32) for _ in range(GROUP_TILES)]

    def constant(values, first, last):
        low, high = float(np.float32(values[first])), float(np.float32(values[last]))
        return low if first == last else jnp.where(upper, low, high)

    for pair in range(BINS // 16):
        both = spectrum_ref[16 * pair : 16 * pair + 16, :].astype(F32)
        for half in range(2):
            t = 2 * pair + half
            p = t % GROUP_TILES
            tile = both[TILE * half : TILE * (half + 1)]
            slope = constant(1.2 / SPEED, *tile_freqs(t))
            weight = constant(stress_coef * AREA * SIGMA / SPEED, *tile_freqs(t))
            grown = jnp.maximum(0.0, slope * along[p] - 1.0)
            totals[p] = totals[p] + (weight * tile) * grown
    return [
        jnp.sum(sum(a * b for a, b in zip(parts, totals)), axis=0, keepdims=True)
        for parts in (cosines, sines)
    ]


def spread_kernel(
    devices, section, order_ref, recv_ref, spectrum_ref, table_ref, angle_ref, out_ref,
    field_a, field_b, wet_ref, numbers_ref, slot_smem,
):
    each, kept, rows = layout(devices)
    ids = row_ids()
    lane = lax.broadcasted_iota(jnp.int32, (TILE, LAT), 1)
    unit = math.gcd(devices, UNROLL)

    def every(body, batch=1):
        if devices == unit:
            for k in range(0, unit, batch):
                body(*range(k, k + batch))
            return

        def some(block, carry):
            for k in range(0, unit, batch):
                body(*(block * unit + k + n for n in range(batch)))
            return carry

        lax.fori_loop(0, devices // unit, some, 0)

    span = min(LAT, devices)
    for block in range(devices // span):

        def place(s, tile, block=block):
            here = recv_ref[block * span + s, kept : kept + TILE, :].astype(F32)
            return jnp.where(lane == s, here, tile)

        orders = lax.fori_loop(0, span, place, jnp.zeros((TILE, LAT), F32), unroll=min(span, UNROLL))
        last = orders[TILE - 1 :].astype(jnp.int32)
        for s in range(span):
            slot_smem[(block * span + s) // section * section + last[0, s]] = block * span + s

    def weather(column):
        tile = recv_ref[column, kept : kept + TILE, :].astype(F32)
        return tile[1:2] + tile[2:3], tile[3:4] + tile[4:5], tile[5:6] + tile[6:7]

    def spread_lane(ref, t, k):
        return jnp.broadcast_to(ref[TILE * t : TILE * (t + 1), k : k + 1], (TILE, LAT))

    for t in range(rows // TILE):
        for k in range(8):
            numbers_ref[k, TILE * t : TILE * (t + 1), :] = spread_lane(table_ref, t, k)
    numbers_ref[6] = jnp.where(lane_whole(rows) == 0, 0.0, numbers_ref[6])
    numbers_ref[7] = jnp.where(lane_whole(rows) == LAT - 1, 0.0, numbers_ref[7])
    base = lax.axis_index("sec") * section
    me = base + lax.axis_index("dom")
    angles = [[spread_lane(angle_ref, p, k) for p in range(GROUP_TILES)] for k in range(2)]
    stress = own_stress(spectrum_ref, *angles, *weather(base + order_ref[0])[:2])
    column_row = jnp.full((1, LAT), order_ref[0], jnp.int32).astype(F32)
    ending = stack_rows([None, stress[0], stress[1], column_row])
    def renew(column):
        east, north, wet = weather(column)
        wet_ref[column] = jnp.broadcast_to(wet, (TILE, LAT))
        energy = recv_ref[slot_smem[column]].astype(F32)
        push = jnp.exp(jnp.maximum(0.0, numbers_ref[0] * east + numbers_ref[1] * north - numbers_ref[2]))
        field_a[column] = wet * energy * push

    every(renew)

    def around(column):
        if isinstance(column, int):
            return (column - 1) % devices, (column + 1) % devices
        return jnp.where(column == 0, devices - 1, column - 1), jnp.where(column == devices - 1, 0, column + 1)

    sure = tile_slots(devices)[1]
    northward = me < devices // 2

    def mover(source, t):
        part = pl.ds(TILE * t, TILE)
        keep, from_west, from_east, from_south, from_north = (numbers_ref[k, part, :] for k in range(3, 8))
        westerly, southerly = from_west > 0.0, from_south > 0.0
        from_x, from_y = from_west + from_east, from_south + from_north
        way = spare_way(devices) if TILE * t == kept else 0
        aside = column_way(devices, t)

        def shifted(here):
            if t < sure:
                return pltpu.roll(here, jnp.where(northward, 1, LAT - 1), 1)
            if way:
                return pltpu.roll(here, way % LAT, 1)
            return jnp.where(southerly, pltpu.roll(here, 1, 1), pltpu.roll(here, LAT - 1, 1))

        def moved(column):
            west, east = around(column)
            here = source[column, part, :]
            if aside:
                beside = source[west if aside > 0 else east, part, :]
            else:
                beside = jnp.where(westerly, source[west, part, :], source[east, part, :])
            total = keep * here + from_x * beside
            return wet_ref[column] * (total + from_y * shifted(here))

        return moved

    for substep in range(SUBSTEPS - 1):
        source, target = (field_a, field_b) if substep % 2 == 0 else (field_b, field_a)
        for t in range(rows // TILE):
            moved = mover(source, t)

            def step(column):
                target[column, TILE * t : TILE * (t + 1), :] = moved(column)

            every(step)

    back = (kept + QUAD) // QUAD
    source = field_a if (SUBSTEPS - 1) % 2 == 0 else field_b
    for t in range(0, rows // TILE, 2):
        upper_tile, lower_tile = mover(source, t), mover(source, t + 1)

        def finish(*columns):
            made = []
            for column in columns:
                upper, lower = upper_tile(column), lower_tile(column)
                if TILE * (t + 1) == kept:
                    lower = jnp.where(ids == 0, lower, ending)
                made.append(jnp.concatenate([upper, lower], axis=0))
            for column, value in zip(columns, made):
                for piece in range(min(4, back - 4 * (t // 2))):
                    quarter = value[QUAD * piece : QUAD * (piece + 1)].astype(BF)
                    out_ref[slot_smem[column], 4 * (t // 2) + piece] = quarter

        every(finish, min(BATCH, unit))


def spread(devices, section, block_order, received, spectrum, table):
    each, kept, rows = layout(devices)
    span = min(LAT, devices)
    return pl.pallas_call(
        functools.partial(spread_kernel, devices, section),
        out_shape=jax.ShapeDtypeStruct((devices, (kept + QUAD) // QUAD, QUAD, LAT), BF),
        in_specs=[smem(), vmem(), vmem(), vmem(), vmem()],
        out_specs=vmem(),
        scratch_shapes=[
            pltpu.VMEM((devices, rows, LAT), F32),
            pltpu.VMEM((devices, rows, LAT), F32),
            pltpu.VMEM((devices, TILE, LAT), F32),
            pltpu.VMEM((8, rows, LAT), F32),
            pltpu.SMEM((devices,), jnp.int32),
        ],
        compiler_params=pltpu.CompilerParams(vmem_limit_bytes=32 << 20),
    )(block_order, received, spectrum, table, jnp.asarray(angle_table()))


def collect(devices, section, returned_ref, wet_ref, stress_ref):
    each, kept, rows = layout(devices)
    base = lax.axis_index("sec") * section
    rank = lax.axis_index("dom").astype(F32)

    def pick(s, total):
        tile = returned_ref[base + s, kept // QUAD].astype(F32)
        mine = jnp.broadcast_to(tile[QUAD - 1 : QUAD] == rank, (QUAD, LAT))
        return jnp.where(mine, tile, total)

    tile = lax.fori_loop(0, section, pick, jnp.zeros((QUAD, LAT), F32), unroll=8)
    stress_ref[...] = wet_ref[0:1, :] * tile[1:3]


def unpack_kernel(devices, section, returned_ref, wet_ref, out_ref, stress_ref):
    each, kept, rows = layout(devices)
    left = BINS - devices * each
    home = {t: (d, k) for d, tiles in enumerate(tile_slots(devices)[0]) for k, t in enumerate(tiles)}
    for pair in range(devices * each // 16):
        both = []
        for d, k in (home[2 * pair], home[2 * pair + 1]):
            both += [returned_ref[d, 2 * k + half].astype(F32) for half in range(2)]
        out_ref[16 * pair : 16 * (pair + 1), :] = jnp.concatenate(both, axis=0).astype(BF)
    spare = []
    for tile in range(left // TILE):
        heads = [returned_ref[TILE * tile + r, kept // QUAD].astype(F32)[:1] for r in range(TILE)]
        spare.append(stack_rows(heads))
    out_ref[devices * each :, :] = jnp.concatenate(spare, axis=0).astype(BF)
    collect(devices, section, returned_ref, wet_ref, stress_ref)


def unpacked(devices, section, returned, wet):
    each, kept, rows = layout(devices)
    left = BINS - devices * each
    stress_shape = jax.ShapeDtypeStruct((2, LAT), F32)
    params = pltpu.CompilerParams(vmem_limit_bytes=24 << 20)
    if each == kept and devices % 2 == 0 and each % TILE == 0 and left % 16 == 0:
        return pl.pallas_call(
            functools.partial(unpack_kernel, devices, section),
            out_shape=(jax.ShapeDtypeStruct((BINS, LAT), BF), stress_shape),
            in_specs=[vmem(), vmem()],
            out_specs=(vmem(), vmem()),
            compiler_params=params,
        )(returned, wet)
    stress = pl.pallas_call(
        functools.partial(collect, devices, section),
        out_shape=stress_shape,
        in_specs=[vmem(), vmem()],
        out_specs=vmem(),
        compiler_params=params,
    )(returned, wet)
    returned = returned.reshape(devices, -1, LAT)
    main = returned[:, :each].reshape(devices * each, LAT)
    return jnp.concatenate([main, returned[:left, kept]], axis=0), stress


def on_device(devices, section, spectrum, surface_wind, wet_mask, block_order):
    wet = wet_mask.reshape(1, LAT)
    sending, table = packed(devices, section, block_order, spectrum, surface_wind, wet)
    received = lax.all_to_all(sending, AXES, split_axis=0, concat_axis=0, tiled=True)
    leaving = spread(devices, section, block_order, received, spectrum, table)
    returned = lax.all_to_all(leaving, AXES, split_axis=0, concat_axis=0, tiled=True)
    return unpacked(devices, section, returned, wet)


def solution(mesh):
    section = mesh.shape["dom"]
    devices = mesh.shape["sec"] * section
    placed = (P(None, AXES), P(None, AXES), P(AXES), P(AXES))
    return jax.shard_map(
        functools.partial(on_device, devices, section),
        mesh=mesh,
        in_specs=placed,
        out_specs=(P(None, AXES), P(None, AXES)),
        check_vma=False,
    )
```

```python
import functools
import math

import jax
import jax.numpy as jnp
import numpy as np
from jax import lax
from jax.experimental import pallas as pl
from jax.experimental.pallas import tpu as pltpu
from jax.sharding import PartitionSpec as P

NF = 36
ND = 36
BINS = NF * ND
LAT = 128
SUBSTEPS = 4

gravity = 9.81
base_freq = 0.035
freq_growth = 1.1
wind_rate = 0.015
dissip_rate = 0.008
steep_ref = 3.0
stress_coef = 0.01
courant = 0.62

AXES = ("sec", "dom")
TILE = 8
QUAD = 4
UNROLL = 32
BATCH = 8
PART = 144
PARTS = BINS // PART
GROUP_TILES = 9
BF = jnp.bfloat16
F32 = jnp.float32

FREQ = np.arange(NF, dtype=np.float64)
SIGMA = 2.0 * math.pi * base_freq * freq_growth**FREQ
WAVENUM = SIGMA * SIGMA / gravity
SPEED = gravity / SIGMA
AREA = 0.1 * SIGMA * (2.0 * math.pi / ND)
THETA = 2.0 * math.pi * np.arange(ND, dtype=np.float64) / ND
COS, SIN = (np.where(np.abs(wave) < 1e-9, 0.0, wave) for wave in (np.cos(THETA), np.sin(THETA)))


def vmem():
    return pl.BlockSpec(memory_space=pltpu.VMEM)


def smem():
    return pl.BlockSpec(memory_space=pltpu.SMEM)


def hbm():
    return pl.BlockSpec(memory_space=pltpu.HBM)


def layout(devices):
    each = BINS // devices
    rows = -(-(each + TILE) // 16) * 16
    return each, rows - TILE, rows


def tile_slots(devices):
    each, kept, rows = layout(devices)
    if each != kept:
        return None, 0
    count, half = each // TILE, devices // 2
    ways = [[], [], []]
    for t in range(devices * count):
        wave = SIN[(TILE * t + np.arange(TILE)) % ND]
        ways[0 if (wave >= 0).all() else 1 if (wave <= 0).all() else 2].append(t)
    def eastward(t):
        return (COS[(TILE * t + np.arange(TILE)) % ND] >= 0).all()

    def westward(t):
        return (COS[(TILE * t + np.arange(TILE)) % ND] <= 0).all()

    ways[0].sort(key=lambda t: (not eastward(t), t))
    ways[1].sort(key=lambda t: (not eastward(t), t))
    sure = min(len(ways[0]) // half, len(ways[1]) // half, count)
    rest = sorted(ways[0][sure * half :] + ways[1][sure * half :] + ways[2], key=lambda t: (not westward(t), t))
    slots = []
    for d in range(devices):
        way, place = ways[d // half], d % half
        slots.append([way[half * k + place] for k in range(sure)] + [rest[devices * k + d] for k in range(count - sure)])
    return slots, sure


def column_way(devices, k):
    slots = tile_slots(devices)[0]
    if slots is None or k >= len(slots[0]):
        return 0
    wave = np.concatenate([COS[(TILE * tiles[k] + np.arange(TILE)) % ND] for tiles in slots])
    return 1 if (wave >= 0).all() else -1 if (wave <= 0).all() else 0


def spare_way(devices):
    wave = SIN[np.arange(BINS // devices * devices, BINS) % ND]
    return 1 if (wave >= 0).all() else -1 if (wave <= 0).all() else 0


def device_tables(devices):
    each, kept, rows = layout(devices)
    slots = tile_slots(devices)[0]
    table = np.zeros((devices, rows, LAT), np.float64)
    for device in range(devices):
        bins = np.full((rows,), -1)
        if slots is None:
            bins[:each] = device * each + np.arange(each)
        else:
            bins[:each] = (TILE * np.array(slots[device])[:, None] + np.arange(TILE)).reshape(-1)
        if devices * each + device < BINS:
            bins[kept] = devices * each + device
        real = bins >= 0
        i, j = np.maximum(bins, 0) // ND, np.maximum(bins, 0) % ND
        scale = wind_rate * SIGMA[i]
        travel = courant * freq_growth ** (-i.astype(np.float64))
        cx, cy = travel * COS[j], travel * SIN[j]
        values = (
            scale * 1.2 / SPEED[i] * COS[j],
            scale * 1.2 / SPEED[i] * SIN[j],
            scale,
            1.0 - np.abs(cx) - np.abs(cy),
            np.maximum(cx, 0.0),
            np.maximum(-cx, 0.0),
            np.maximum(cy, 0.0),
            np.maximum(-cy, 0.0),
        )
        for lane, value in enumerate(values):
            table[device, :, lane] = np.where(real, value, 0.0)
    return table.astype(np.float32)


def angle_table():
    table = np.zeros((GROUP_TILES * TILE, LAT), np.float64)
    angle = np.arange(GROUP_TILES * TILE) % ND
    table[:, 0], table[:, 1] = COS[angle], SIN[angle]
    return table.astype(np.float32)


def split(value):
    high = value.astype(BF)
    return high.astype(F32), (value - high.astype(F32)).astype(BF).astype(F32)


def row_ids():
    return lax.broadcasted_iota(jnp.int32, (TILE, LAT), 0)


def stack_rows(rows):
    ids = row_ids()
    tile = jnp.zeros((TILE, LAT), F32)
    for r, row in enumerate(rows):
        if row is not None:
            tile = jnp.where(ids == r, jnp.broadcast_to(row, (TILE, LAT)), tile)
    return tile


def tile_freqs(t):
    return (TILE * t) // ND, (TILE * t + TILE - 1) // ND


def decayed_tiles(spectrum_ref, arrive):
    ids = row_ids()
    upper = ids < TILE // 2
    tiles = []
    sums = [jnp.zeros((TILE, LAT), F32) for _ in range(3)]
    for group in range(NF // 2):
        if group % 2 == 0:
            arrive(group // 2)
            for pair in range(GROUP_TILES):
                first = PART * (group // 2) + 16 * pair
                both = spectrum_ref[first : first + 16, :].astype(F32)
                tiles += [both[:TILE], both[TILE:]]
        nine = tiles[GROUP_TILES * group : GROUP_TILES * (group + 1)]
        low = (nine[0] + nine[1]) + (nine[2] + nine[3]) + jnp.where(upper, nine[4], 0.0)
        high = (nine[5] + nine[6]) + (nine[7] + nine[8]) + jnp.where(upper, 0.0, nine[4])
        for i, part in ((2 * group, low), (2 * group + 1, high)):
            weights = (AREA[i], AREA[i] / SIGMA[i], AREA[i] / math.sqrt(WAVENUM[i]))
            sums = [s + float(np.float32(w)) * part for s, w in zip(sums, weights)]
    moments = [jnp.broadcast_to(jnp.sum(s, axis=0, keepdims=True), (TILE, LAT)) for s in sums]
    mean_freq = moments[0] / moments[1]
    mean_wavenum = (moments[0] / moments[2]) ** 2
    steepness = moments[0] * mean_wavenum * mean_wavenum
    strength = mean_freq * (steepness / steep_ref) ** 2
    inverse = 1.0 / mean_wavenum
    factors = []
    for i in range(NF):
        ratio = float(np.float32(WAVENUM[i])) * inverse
        factors.append(jnp.exp(-dissip_rate * (strength * (0.5 * ratio + 0.5 * ratio * ratio))))

    def decayed(t):
        first, last = tile_freqs(t)
        factor = factors[first]
        if last != first:
            factor = jnp.where(upper, factor, factors[last])
        return spectrum_ref[TILE * t : TILE * (t + 1), :].astype(F32) * factor

    return decayed


def shared_tile(wind_ref, wet_ref, order):
    east, north, wet = split(wind_ref[0:1, :]), split(wind_ref[1:2, :]), split(wet_ref[0:1, :])
    column = jnp.full((1, LAT), order, jnp.int32).astype(F32)
    return stack_rows([None, *east, *north, *wet, column])


def fetch(section, spectrum_hbm, wind_hbm, wet_hbm, tables_hbm, spectrum_ref, wind_ref, wet_ref, table_ref, sems):
    me = lax.axis_index("sec") * section + lax.axis_index("dom")
    parts = [
        pltpu.make_async_copy(
            spectrum_hbm.at[pl.ds(PART * k, PART), :], spectrum_ref.at[pl.ds(PART * k, PART), :], sems.at[k]
        )
        for k in range(PARTS)
    ]
    rest = [
        pltpu.make_async_copy(source, target, sems.at[PARTS + k])
        for k, (source, target) in enumerate(
            ((wind_hbm, wind_ref), (wet_hbm, wet_ref), (tables_hbm.at[me], table_ref))
        )
    ]
    for copy in parts + rest:
        copy.start()

    def arrive(part):
        parts[part].wait()

    def arrive_rest():
        for copy in rest:
            copy.wait()

    return arrive, arrive_rest


def pack_kernel(
    devices, section, order_ref, spectrum_hbm, wind_hbm, wet_hbm, tables_hbm, out_ref, table_ref,
    spectrum_ref, wind_ref, wet_ref, sems,
):
    each, kept, rows = layout(devices)
    arrive, arrive_rest = fetch(
        section, spectrum_hbm, wind_hbm, wet_hbm, tables_hbm, spectrum_ref, wind_ref, wet_ref, table_ref, sems
    )
    decayed = decayed_tiles(spectrum_ref, arrive)
    arrive_rest()
    shared = shared_tile(wind_ref, wet_ref, order_ref[0])
    first = row_ids() == 0
    left = BINS - devices * each
    slots = tile_slots(devices)[0]
    spares = [decayed(t) for t in range(devices * each // TILE, BINS // TILE)]
    for d in range(devices):
        last = shared
        if d < left:
            row = spares[d // TILE][d % TILE : d % TILE + 1]
            last = jnp.where(first, jnp.broadcast_to(row, (TILE, LAT)), shared)
        chunk = jnp.concatenate([decayed(t) for t in slots[d]] + [last], axis=0)
        out_ref[d] = chunk.astype(BF)


def loose_kernel(
    section, order_ref, spectrum_hbm, wind_hbm, wet_hbm, tables_hbm, out_ref, table_ref, shared_ref,
    spectrum_ref, wind_ref, wet_ref, sems,
):
    arrive, arrive_rest = fetch(
        section, spectrum_hbm, wind_hbm, wet_hbm, tables_hbm, spectrum_ref, wind_ref, wet_ref, table_ref, sems
    )
    decayed = decayed_tiles(spectrum_ref, arrive)
    arrive_rest()
    for pair in range(BINS // 16):
        both = jnp.concatenate([decayed(2 * pair), decayed(2 * pair + 1)], axis=0)
        out_ref[16 * pair : 16 * pair + 16, :] = both.astype(BF)
    shared_ref[...] = shared_tile(wind_ref, wet_ref, order_ref[0])


def packed(devices, section, block_order, spectrum, surface_wind, wet):
    each, kept, rows = layout(devices)
    shape = jax.ShapeDtypeStruct((devices, rows, LAT), BF)
    table_shape = jax.ShapeDtypeStruct((rows, LAT), F32)
    shared = dict(
        in_specs=[smem(), hbm(), hbm(), hbm(), hbm()],
        scratch_shapes=[
            pltpu.VMEM((BINS, LAT), BF),
            pltpu.VMEM((2, LAT), F32),
            pltpu.VMEM((1, LAT), F32),
            pltpu.SemaphoreType.DMA((PARTS + 3,)),
        ],
        compiler_params=pltpu.CompilerParams(vmem_limit_bytes=24 << 20),
    )
    stay = (spectrum, surface_wind, wet, jnp.asarray(device_tables(devices)))
    operands = (block_order, *(pltpu.with_memory_space_constraint(array, pltpu.HBM) for array in stay))
    if each == kept:
        return pl.pallas_call(
            functools.partial(pack_kernel, devices, section),
            out_shape=(shape, table_shape),
            out_specs=(vmem(), vmem()),
            **shared,
        )(*operands)
    decayed, table, tile = pl.pallas_call(
        functools.partial(loose_kernel, section),
        out_shape=(
            jax.ShapeDtypeStruct((BINS, LAT), BF),
            table_shape,
            jax.ShapeDtypeStruct((TILE, LAT), F32),
        ),
        out_specs=(vmem(), vmem(), vmem()),
        **shared,
    )(*operands)
    main = decayed[: devices * each].reshape(devices, each, LAT)
    main = jnp.pad(main, ((0, 0), (0, kept - each), (0, 0)))
    spare = decayed[devices * each :]
    spare = jnp.pad(spare, ((0, devices - spare.shape[0]), (0, 0)))[:, None]
    common = jnp.broadcast_to(tile[1:].astype(BF)[None], (devices, TILE - 1, LAT))
    return jnp.concatenate([main, spare, common], axis=1), table


def lane_whole(rows):
    return lax.broadcasted_iota(jnp.int32, (rows, LAT), 1)


def own_stress(spectrum_ref, cosines, sines, east, north):
    upper = row_ids() < TILE // 2
    along = [c * east + s * north for c, s in zip(cosines, sines)]
    totals = [jnp.zeros((TILE, LAT), F32) for _ in range(GROUP_TILES)]

    def constant(values, first, last):
        low, high = float(np.float32(values[first])), float(np.float32(values[last]))
        return low if first == last else jnp.where(upper, low, high)

    for pair in range(BINS // 16):
        both = spectrum_ref[16 * pair : 16 * pair + 16, :].astype(F32)
        for half in range(2):
            t = 2 * pair + half
            p = t % GROUP_TILES
            tile = both[TILE * half : TILE * (half + 1)]
            slope = constant(1.2 / SPEED, *tile_freqs(t))
            weight = constant(stress_coef * AREA * SIGMA / SPEED, *tile_freqs(t))
            grown = jnp.maximum(0.0, slope * along[p] - 1.0)
            totals[p] = totals[p] + (weight * tile) * grown
    return [
        jnp.sum(sum(a * b for a, b in zip(parts, totals)), axis=0, keepdims=True)
        for parts in (cosines, sines)
    ]


def spread_kernel(
    devices, section, order_ref, recv_ref, spectrum_ref, table_ref, angle_ref, out_ref,
    field_a, field_b, wet_ref, numbers_ref, slot_smem,
):
    each, kept, rows = layout(devices)
    ids = row_ids()
    lane = lax.broadcasted_iota(jnp.int32, (TILE, LAT), 1)
    unit = math.gcd(devices, UNROLL)

    def every(body, batch=1):
        if devices == unit:
            for k in range(0, unit, batch):
                body(*range(k, k + batch))
            return

        def some(block, carry):
            for k in range(0, unit, batch):
                body(*(block * unit + k + n for n in range(batch)))
            return carry

        lax.fori_loop(0, devices // unit, some, 0)

    span = min(LAT, devices)
    for block in range(devices // span):

        def place(s, tile, block=block):
            here = recv_ref[block * span + s, kept : kept + TILE, :].astype(F32)
            return jnp.where(lane == s, here, tile)

        orders = lax.fori_loop(0, span, place, jnp.zeros((TILE, LAT), F32), unroll=min(span, UNROLL))
        last = orders[TILE - 1 :].astype(jnp.int32)
        for s in range(span):
            slot_smem[(block * span + s) // section * section + last[0, s]] = block * span + s

    def weather(column):
        tile = recv_ref[column, kept : kept + TILE, :].astype(F32)
        return tile[1:2] + tile[2:3], tile[3:4] + tile[4:5], tile[5:6] + tile[6:7]

    def spread_lane(ref, t, k):
        return jnp.broadcast_to(ref[TILE * t : TILE * (t + 1), k : k + 1], (TILE, LAT))

    for t in range(rows // TILE):
        for k in range(8):
            numbers_ref[k, TILE * t : TILE * (t + 1), :] = spread_lane(table_ref, t, k)
    numbers_ref[6] = jnp.where(lane_whole(rows) == 0, 0.0, numbers_ref[6])
    numbers_ref[7] = jnp.where(lane_whole(rows) == LAT - 1, 0.0, numbers_ref[7])
    base = lax.axis_index("sec") * section
    me = base + lax.axis_index("dom")
    angles = [[spread_lane(angle_ref, p, k) for p in range(GROUP_TILES)] for k in range(2)]
    stress = own_stress(spectrum_ref, *angles, *weather(base + order_ref[0])[:2])
    column_row = jnp.full((1, LAT), order_ref[0], jnp.int32).astype(F32)
    ending = stack_rows([None, stress[0], stress[1], column_row])
    def renew(column):
        east, north, wet = weather(column)
        wet_ref[column] = jnp.broadcast_to(wet, (TILE, LAT))
        energy = recv_ref[slot_smem[column]].astype(F32)
        push = jnp.exp(jnp.maximum(0.0, numbers_ref[0] * east + numbers_ref[1] * north - numbers_ref[2]))
        field_a[column] = wet * energy * push

    every(renew)

    def around(column):
        if isinstance(column, int):
            return (column - 1) % devices, (column + 1) % devices
        return jnp.where(column == 0, devices - 1, column - 1), jnp.where(column == devices - 1, 0, column + 1)

    sure = tile_slots(devices)[1]
    northward = me < devices // 2

    def mover(source, t):
        part = pl.ds(TILE * t, TILE)
        keep, from_west, from_east, from_south, from_north = (numbers_ref[k, part, :] for k in range(3, 8))
        westerly, southerly = from_west > 0.0, from_south > 0.0
        from_x, from_y = from_west + from_east, from_south + from_north
        way = spare_way(devices) if TILE * t == kept else 0
        aside = column_way(devices, t)

        def shifted(here):
            if t < sure:
                return pltpu.roll(here, jnp.where(northward, 1, LAT - 1), 1)
            if way:
                return pltpu.roll(here, way % LAT, 1)
            return jnp.where(southerly, pltpu.roll(here, 1, 1), pltpu.roll(here, LAT - 1, 1))

        held = {}

        def load(column):
            if not isinstance(column, int):
                return source[column, part, :]
            if column not in held:
                held[column] = source[column, part, :]
            return held[column]

        def moved(column):
            west, east = around(column)
            here = load(column)
            if aside:
                beside = load(west if aside > 0 else east)
            else:
                beside = jnp.where(westerly, load(west), load(east))
            total = keep * here + from_x * beside
            return wet_ref[column] * (total + from_y * shifted(here))

        return moved

    for substep in range(SUBSTEPS - 1):
        source, target = (field_a, field_b) if substep % 2 == 0 else (field_b, field_a)
        for t in range(rows // TILE):
            moved = mover(source, t)

            def step(column):
                target[column, TILE * t : TILE * (t + 1), :] = moved(column)

            every(step)

    back = (kept + QUAD) // QUAD
    source = field_a if (SUBSTEPS - 1) % 2 == 0 else field_b
    for t in range(0, rows // TILE, 2):
        upper_tile, lower_tile = mover(source, t), mover(source, t + 1)

        def finish(*columns):
            made = []
            for column in columns:
                upper, lower = upper_tile(column), lower_tile(column)
                if TILE * (t + 1) == kept:
                    lower = jnp.where(ids == 0, lower, ending)
                made.append(jnp.concatenate([upper, lower], axis=0))
            for column, value in zip(columns, made):
                for piece in range(min(4, back - 4 * (t // 2))):
                    quarter = value[QUAD * piece : QUAD * (piece + 1)].astype(BF)
                    out_ref[slot_smem[column], 4 * (t // 2) + piece] = quarter

        every(finish, min(BATCH, unit))


def spread(devices, section, block_order, received, spectrum, table):
    each, kept, rows = layout(devices)
    span = min(LAT, devices)
    return pl.pallas_call(
        functools.partial(spread_kernel, devices, section),
        out_shape=jax.ShapeDtypeStruct((devices, (kept + QUAD) // QUAD, QUAD, LAT), BF),
        in_specs=[smem(), vmem(), vmem(), vmem(), vmem()],
        out_specs=vmem(),
        scratch_shapes=[
            pltpu.VMEM((devices, rows, LAT), F32),
            pltpu.VMEM((devices, rows, LAT), F32),
            pltpu.VMEM((devices, TILE, LAT), F32),
            pltpu.VMEM((8, rows, LAT), F32),
            pltpu.SMEM((devices,), jnp.int32),
        ],
        compiler_params=pltpu.CompilerParams(vmem_limit_bytes=32 << 20),
    )(block_order, received, spectrum, table, jnp.asarray(angle_table()))


def collect(devices, section, returned_ref, wet_ref, stress_ref):
    each, kept, rows = layout(devices)
    base = lax.axis_index("sec") * section
    rank = lax.axis_index("dom").astype(F32)

    def pick(s, total):
        tile = returned_ref[base + s, kept // QUAD].astype(F32)
        mine = jnp.broadcast_to(tile[QUAD - 1 : QUAD] == rank, (QUAD, LAT))
        return jnp.where(mine, tile, total)

    tile = lax.fori_loop(0, section, pick, jnp.zeros((QUAD, LAT), F32), unroll=8)
    stress_ref[...] = wet_ref[0:1, :] * tile[1:3]


def unpack_kernel(devices, section, returned_ref, wet_ref, out_ref, stress_ref):
    each, kept, rows = layout(devices)
    left = BINS - devices * each
    home = {t: (d, k) for d, tiles in enumerate(tile_slots(devices)[0]) for k, t in enumerate(tiles)}
    for pair in range(devices * each // 16):
        both = []
        for d, k in (home[2 * pair], home[2 * pair + 1]):
            both += [returned_ref[d, 2 * k + half].astype(F32) for half in range(2)]
        out_ref[16 * pair : 16 * (pair + 1), :] = jnp.concatenate(both, axis=0).astype(BF)
    spare = []
    for tile in range(left // TILE):
        heads = [returned_ref[TILE * tile + r, kept // QUAD].astype(F32)[:1] for r in range(TILE)]
        spare.append(stack_rows(heads))
    out_ref[devices * each :, :] = jnp.concatenate(spare, axis=0).astype(BF)
    collect(devices, section, returned_ref, wet_ref, stress_ref)


def unpacked(devices, section, returned, wet):
    each, kept, rows = layout(devices)
    left = BINS - devices * each
    stress_shape = jax.ShapeDtypeStruct((2, LAT), F32)
    params = pltpu.CompilerParams(vmem_limit_bytes=24 << 20)
    if each == kept and devices % 2 == 0 and each % TILE == 0 and left % 16 == 0:
        return pl.pallas_call(
            functools.partial(unpack_kernel, devices, section),
            out_shape=(jax.ShapeDtypeStruct((BINS, LAT), BF), stress_shape),
            in_specs=[vmem(), vmem()],
            out_specs=(vmem(), vmem()),
            compiler_params=params,
        )(returned, wet)
    stress = pl.pallas_call(
        functools.partial(collect, devices, section),
        out_shape=stress_shape,
        in_specs=[vmem(), vmem()],
        out_specs=vmem(),
        compiler_params=params,
    )(returned, wet)
    returned = returned.reshape(devices, -1, LAT)
    main = returned[:, :each].reshape(devices * each, LAT)
    return jnp.concatenate([main, returned[:left, kept]], axis=0), stress


def on_device(devices, section, spectrum, surface_wind, wet_mask, block_order):
    wet = wet_mask.reshape(1, LAT)
    sending, table = packed(devices, section, block_order, spectrum, surface_wind, wet)
    received = lax.all_to_all(sending, AXES, split_axis=0, concat_axis=0, tiled=True)
    leaving = spread(devices, section, block_order, received, spectrum, table)
    returned = lax.all_to_all(leaving, AXES, split_axis=0, concat_axis=0, tiled=True)
    return unpacked(devices, section, returned, wet)


def solution(mesh):
    section = mesh.shape["dom"]
    devices = mesh.shape["sec"] * section
    placed = (P(None, AXES), P(None, AXES), P(AXES), P(AXES))
    return jax.shard_map(
        functools.partial(on_device, devices, section),
        mesh=mesh,
        in_specs=placed,
        out_specs=(P(None, AXES), P(None, AXES)),
        check_vma=False,
    )
```
